32 devices in a mesh: dates: 2 (over y), az: 16 (over z, x, core).
Axes of the slice: x: 2, y: 2, z: 4, core: 2. Of those that a mesh axis runs over, the one named last changes fastest.
Arguments:
- secondary_pieces: bfloat16 [4096, 2, 16, 256], P(('dates', 'az')), parts along dimension 0, may hold values from -6 to 6
- piece_target: int32 [4096, 1], P(('dates', 'az')), parts along dimension 0, may hold values from 0 to 15; in each aligned block of 128 rows (0 to 127, 128 to 255, ...) at most 16 rows name the same one
- piece_block: int32 [4096], P(('dates', 'az')), parts along dimension 0, may hold values from 0 to 63
- piece_row: int32 [4096], P(('dates', 'az')), parts along dimension 0, may hold values from 0 to 248
- piece_column: int32 [4096], P(('dates', 'az')), parts along dimension 0, may hold values from -4 to 4
- ramp_rate: float32 [32, 256], P(('dates', 'az')), parts along dimension 0, may hold values from 20 to 200
- centroid: float32 [32, 256], P(('dates', 'az')), parts along dimension 0, may hold values from -8 to 8
- sinc_blocks: float32 [64, 8, 8], replicated, may hold values from -0.75 to 0.75
- reference_tile: float32 [2, 8192, 256], P(None, ('dates', 'az')), parts along dimension 1, may hold values from -6 to 6
- intersection_rows: int32 [32], P(('dates', 'az')), parts along dimension 0, may hold values from 16 to 32, as said below
Outputs:
- coregistered: bfloat16 [4096, 2, 8, 256], P(('dates', 'az')), parts along dimension 0
- interferogram: float32 [2, 8192, 256], P(None, ('dates', 'az')), parts along dimension 1
- diversity_sum: float32 [32, 2, 256], P(('dates', 'az')), parts along dimension 0
The draws below stay inside these ranges and needn't reach their ends.
There are 2 independent parts, one for each index of `dates`. The reference program is written for one: setup_inputs(seed, part) draws one part's arguments, and reference() takes and returns one part's arrays. A program takes and returns all parts, laid end to end along the dimension named above; an argument that names none is the same for every part. Nothing has to cross between parts.
Inputs may be any that keep to these rules, and one draw needn't show every extreme that they name: `piece_target`: of the 128 pieces of one device at most 16 land in the same tile, and in every draw some device sends exactly 16 to one tile. `intersection_rows`: some tile shares exactly 32 lines.
All inputs are finite; a program needn't handle non-finite values.
Results may differ from the reference program's by a relative error of at most 0.0076.
Values may be sent and summed in bfloat16 or wider, within the bound.
A program may use at most 128 MiB of HBM per device.

```python
import math
import jax
import jax.numpy as jnp
import numpy as np
from jax import lax

RANGE_COLS = 256
TILE_ROWS = 256
PIECES = 128
PIECE_ROWS = 8
INTERSECTION = 32
WEIGHT_BLOCKS = 64
CAPACITY = 16
N_AZ = 16


def draw_intersection_rows(key, part):
    key = jax.random.fold_in(key, 7)
    first_key, second_key = jax.random.split(key)
    lengths_drawn = jax.random.randint(first_key, (N_AZ,), INTERSECTION // 2, INTERSECTION + 1).astype(jnp.int32)
    chosen = jax.random.randint(second_key, (), 0, N_AZ)
    return jnp.where(jnp.arange(N_AZ) == chosen, INTERSECTION, lengths_drawn).astype(jnp.int32)


def with_ends(result, stream_key, least, top_value):
    extent = result.shape
    place = [jax.random.randint(jax.random.fold_in(stream_key, axis), (), 0, extent[axis]) for axis in range(len(extent))]
    result = result.at[tuple(place)].set(least)
    longest = extent.index(max(extent))
    place[longest] = (place[longest] + 1) % extent[longest]
    return result.at[tuple(place)].set(top_value)


def block_levels(own_key, dims, cuts, low, largest):
    def one(dim, blocks):
        heights = jax.random.uniform(jax.random.fold_in(jax.random.fold_in(own_key, 6), dim), (blocks,), jnp.float32, low / len(cuts), largest / len(cuts))
        return jnp.repeat(jnp.exp(heights), dims[dim] // blocks).reshape((-1,) + (1,) * (len(dims) - dim - 1))

    factor_of = one(*cuts[0])
    for cut in cuts[1:]:
        factor_of = factor_of * one(*cut)
    return factor_of


def assign_block(own_key, own, number, rows, amount, top, limit, lean):
    ranking = jax.random.permutation(own_key, amount)
    packed, ordinary = load_shares(amount, rows * top, limit, lean, True), load_shares(amount, rows * top, limit, lean, False)
    places = jnp.arange(amount)

    def named(sizes, rotation):
        used = int((sizes > 0).sum())
        fixed = max(1, used // 4)
        passed = fixed + (places - fixed + rotation * (used - fixed)) % max(1, amount - fixed)
        return jnp.zeros((amount,), jnp.int32).at[ranking[jnp.where(places < fixed, places, passed)]].set(jnp.asarray(sizes, jnp.int32))

    sizes = jnp.where(number % 4 == 0, named(packed, number // 4), named(ordinary, number - number // 4 - 1))
    mixed = jax.random.permutation(jax.random.fold_in(own, 3), amount)
    source_of, taker = mixed[0:amount // 2 * 2:2], mixed[1:amount // 2 * 2:2]
    margin = jnp.minimum(sizes[source_of] - 1, limit - sizes[taker]) // 2
    margin = jnp.where((source_of == ranking[0]) | (taker == ranking[0]) | (sizes[taker] == 0), 0, jnp.maximum(margin, 0))
    passed = jax.random.randint(jax.random.fold_in(own, 4), (amount // 2,), 0, 1 << 20) % (margin + 1)
    sizes = sizes.at[source_of].add(-passed).at[taker].add(passed)
    members = jnp.searchsorted(jnp.cumsum(sizes), jnp.arange(rows * top), side="right").astype(jnp.int32)
    listing = members.reshape(top, rows).T
    listing = listing[jax.random.permutation(jax.random.fold_in(own, 1), rows)]
    rotation = jax.random.randint(jax.random.fold_in(own, 2), (rows, 1), 0, top)
    return jnp.take_along_axis(listing, (jnp.arange(top)[None, :] + rotation) % top, axis=1)


def load_shares(amount, total, most, lean, full):
    portions = [(1 << 20) // math.isqrt(standing ** lean) + 1 for standing in range(1, amount + 1)]
    largest = most if full else min(most, max(-(-total // amount), total * portions[0] // sum(portions)))
    least = 1 if total - largest >= amount - 1 else 0
    counts, rest = [largest] + [least] * (amount - 1), total - largest - least * (amount - 1)
    while rest > 0:
        free = [i for i in range(1, amount) if counts[i] < largest] or [i for i in range(1, amount) if counts[i] < most]
        mass, budget = sum([portions[i] for i in free]), rest
        for i in free:
            more = min(most - counts[i], max(1, budget * portions[i] // mass), rest)
            counts[i] = counts[i] + more
            rest = rest - more
    return np.array(counts)


def centred(rng, shape, scale, reach, cuts=(), held_as=jnp.bfloat16):
    factor_of = block_levels(rng, shape, cuts, -0.22, 0.18) if cuts else 1.0
    entries = jax.random.normal(rng, shape, jnp.float32) * scale * factor_of
    return jnp.minimum(jnp.maximum(entries, -reach), reach).astype(held_as)


def setup_inputs(seed: int = 0, part: int = 0) -> dict:
    key_list = jax.random.split(jax.random.key(seed), 11)
    own_keys = jax.random.split(jax.random.fold_in(key_list[10], part), 11)
    secondary_pieces = centred(own_keys[0], (N_AZ * PIECES, 2, PIECE_ROWS + 8, RANGE_COLS), 1.0, 6.0, ((0, 16),))
    piece_target_keys = jax.random.split(jax.random.fold_in(own_keys[1], 1), (N_AZ * PIECES) // PIECES)
    piece_target_turns = jax.random.permutation(jax.random.fold_in(own_keys[1], 3), (N_AZ * PIECES) // PIECES)
    piece_target = jax.vmap(lambda own, number: assign_block(jax.random.fold_in(own_keys[1], 2), own, number, PIECES, N_AZ, 1, CAPACITY, 2))(piece_target_keys, piece_target_turns).reshape((N_AZ * PIECES, 1))
    piece_block = with_ends(jax.random.randint(own_keys[2], (N_AZ * PIECES,), 0, WEIGHT_BLOCKS), jax.random.fold_in(own_keys[2], 1), 0, WEIGHT_BLOCKS - 1).astype(jnp.int32)
    piece_row = with_ends(jax.random.randint(own_keys[3], (N_AZ * PIECES,), 0, TILE_ROWS - PIECE_ROWS + 1), jax.random.fold_in(own_keys[3], 1), 0, TILE_ROWS - PIECE_ROWS).astype(jnp.int32)
    piece_column = with_ends(jax.random.randint(own_keys[4], (N_AZ * PIECES,), -4, 5), jax.random.fold_in(own_keys[4], 1), -4, 4).astype(jnp.int32)
    ramp_rate = jnp.clip(jnp.exp(math.log(200.0) - 2.3025851 * jax.random.uniform(own_keys[5], (N_AZ, RANGE_COLS), jnp.float32) ** block_levels(own_keys[5], (N_AZ, RANGE_COLS), ((0, 16),), -0.2, 0.2)), 20.0, 200.0)
    centroid = jnp.clip(jax.random.uniform(own_keys[6], (N_AZ, RANGE_COLS), jnp.float32, -8.0, 8.0) * block_levels(own_keys[6], (N_AZ, RANGE_COLS), ((0, 16),), -0.4, 0.0), -8.0, 8.0)
    sinc_blocks = centred(key_list[7], (WEIGHT_BLOCKS, 8, 8), 64 ** -0.5, 0.75, (), jnp.float32)
    reference_tile = centred(own_keys[8], (2, N_AZ * TILE_ROWS, RANGE_COLS), 1.0, 6.0, ((1, 16),), jnp.float32)
    intersection_rows = draw_intersection_rows(jax.random.fold_in(jax.random.fold_in(key_list[10], part), 71), part)
    return {"secondary_pieces": secondary_pieces, "piece_target": piece_target, "piece_block": piece_block, "piece_row": piece_row, "piece_column": piece_column, "ramp_rate": ramp_rate, "centroid": centroid, "sinc_blocks": sinc_blocks, "reference_tile": reference_tile, "intersection_rows": intersection_rows}


def ramp_phase(row_times, rate_table, centroid_table):
    scaled = ((row_times - 0.5 * TILE_ROWS) / TILE_ROWS)[:, :, None]
    return jnp.pi * rate_table[:, None, :] * scaled * scaled + 2.0 * jnp.pi * centroid_table[:, None, :] * scaled


def resample_group(pieces, block_index, row_start, col_shift, rate_table, centroid_table, sinc_blocks):
    total = pieces.shape[0]
    width = pieces.shape[3]
    in_rows = pieces.shape[2]
    out_rows = in_rows - 8
    row_float = row_start.astype(jnp.float32)[:, None]
    phase_in = ramp_phase(row_float + jnp.arange(in_rows, dtype=jnp.float32)[None, :] - 3.0, rate_table, centroid_table)
    cosine = jnp.cos(phase_in)
    sine_part = jnp.sin(phase_in)
    real_part = pieces[:, 0].astype(jnp.float32)
    imag_part = pieces[:, 1].astype(jnp.float32)
    deramped = jnp.stack([real_part * cosine + imag_part * sine_part, imag_part * cosine - real_part * sine_part], axis=1)
    deramped = lax.optimization_barrier(deramped.astype(jnp.bfloat16)).astype(jnp.float32)
    padded = jnp.pad(deramped, ((0, 0), (0, 0), (0, 0), (8, 8)))
    window = jax.vmap(lambda item, begin_at: lax.dynamic_slice_in_dim(item, begin_at, width + 7, 2))(padded, (col_shift + 5).astype(jnp.int32))
    stacked = jnp.stack([window[..., tap_index:tap_index + width] for tap_index in range(8)], axis=2)
    stacked = stacked.reshape(total, 2, 8 * in_rows, width)
    selected = sinc_blocks[block_index]
    shifter = (jnp.arange(in_rows)[None, None, :] == jnp.arange(out_rows)[None, :, None] + jnp.arange(8)[:, None, None]).astype(jnp.float32)
    band_matrix = jnp.einsum("nab,arq->nrbq", selected, shifter, precision=lax.Precision.HIGHEST).reshape(total, out_rows, 8 * in_rows)
    band_matrix = lax.optimization_barrier(band_matrix.astype(jnp.bfloat16)).astype(jnp.float32)
    interpolated = jnp.einsum("nrk,nzkc->nzrc", band_matrix, stacked, precision=lax.Precision.HIGHEST)
    out_times = row_float + jnp.arange(out_rows, dtype=jnp.float32)[None, :] + block_index.astype(jnp.float32)[:, None] / WEIGHT_BLOCKS
    phase_out = ramp_phase(out_times, rate_table, centroid_table)
    cosine_out = jnp.cos(phase_out)
    sine_out = jnp.sin(phase_out)
    out_real = interpolated[:, 0] * cosine_out - interpolated[:, 1] * sine_out
    out_imag = interpolated[:, 1] * cosine_out + interpolated[:, 0] * sine_out
    return jnp.stack([out_real, out_imag], axis=1).astype(jnp.bfloat16)


def reference(secondary_pieces, piece_target, piece_block, piece_row, piece_column, ramp_rate, centroid, sinc_blocks, reference_tile, intersection_rows):
    target = piece_target[:, 0]

    def per_source(bundle):
        pieces, targets, blocks, rows_here, columns = bundle
        return resample_group(pieces, blocks, rows_here, columns, ramp_rate[targets], centroid[targets], sinc_blocks)

    def shaped(array_item):
        return array_item.reshape((N_AZ, PIECES) + array_item.shape[1:])

    coregistered = lax.map(per_source, (shaped(secondary_pieces), shaped(target), shaped(piece_block), shaped(piece_row), shaped(piece_column)))
    coregistered = coregistered.reshape(N_AZ * PIECES, 2, PIECE_ROWS, RANGE_COLS)
    image_lines = target[:, None] * TILE_ROWS + piece_row[:, None] + jnp.arange(PIECE_ROWS, dtype=jnp.int32)[None, :]
    values = jnp.transpose(coregistered.astype(jnp.float32), (0, 2, 1, 3))
    assembled = jnp.zeros((N_AZ * TILE_ROWS, 2, RANGE_COLS), jnp.float32).at[image_lines].add(values)
    assembled = jnp.transpose(assembled, (1, 0, 2))
    inter_real = reference_tile[0] * assembled[0] + reference_tile[1] * assembled[1]
    inter_imag = reference_tile[1] * assembled[0] - reference_tile[0] * assembled[1]
    interferogram = jnp.stack([inter_real, inter_imag], axis=0)
    shaped_ifg = interferogram.reshape(2, N_AZ, TILE_ROWS, RANGE_COLS)
    head_rows = shaped_ifg[:, :, :INTERSECTION]
    tail_rows = shaped_ifg[:, :, TILE_ROWS - INTERSECTION:]
    previous = jnp.concatenate([jnp.zeros_like(tail_rows[:, :1]), tail_rows[:, :-1]], axis=1)
    positions = jnp.arange(INTERSECTION, dtype=jnp.int32)
    aligned_index = (positions[None, :] + INTERSECTION - intersection_rows[:, None]) % INTERSECTION
    aligned = jnp.take_along_axis(previous, aligned_index[None, :, :, None], axis=2)
    row_mask = (positions[None, :] < intersection_rows[:, None]).astype(jnp.float32)[:, :, None]
    product_real = jnp.sum((head_rows[0] * aligned[0] + head_rows[1] * aligned[1]) * row_mask, axis=1)
    product_imag = jnp.sum((head_rows[1] * aligned[0] - head_rows[0] * aligned[1]) * row_mask, axis=1)
    lengths_float = intersection_rows.astype(jnp.float32)[:, None]
    diversity_sum = jnp.stack([product_real / lengths_float, product_imag / lengths_float], axis=1)
    return coregistered, interferogram, diversity_sum
```

```python
import functools

import jax
import jax.numpy as jnp
from jax import lax
from jax.experimental import pallas as pl
from jax.experimental.pallas import tpu as pltpu
from jax.sharding import PartitionSpec as P

TILE_ROWS = 256
INTERSECTION = 32
WEIGHT_BLOCKS = 64
GROUP = 16
MESH = pl.DeviceIdType.MESH

SIN_FIT = (6.2831807136535645, -41.33925247192383, 81.40833282470703, -71.61119079589844)
COS_FIT = (0.9999932646751404, -19.73573875427246, 64.65997314453125, -78.21002960205078)


def unit_phasor(turns):
    part = turns - jnp.round(turns)
    w = 0.25 - jnp.abs(part)
    w2 = w * w
    even = jnp.full_like(w2, COS_FIT[-1])
    for coeff in COS_FIT[-2::-1]:
        even = even * w2 + coeff
    odd = jnp.full_like(w2, SIN_FIT[-1])
    for coeff in SIN_FIT[-2::-1]:
        odd = odd * w2 + coeff
    return odd * w, jnp.where(part < 0, -even, even)


def resample_kernel(
    capacity,
    target,
    block,
    row,
    col,
    x_ref,
    table_ref,
    taps_ref,
    out_ref,
    message_ref,
    lines_ref,
    deramped,
    band,
    mixed,
    used,
):
    step = pl.program_id(0)
    width = x_ref.shape[3]
    half = width // 2

    @pl.when(step == 0)
    def _():
        message_ref[...] = jnp.zeros_like(message_ref)
        lines_ref[...] = jnp.full_like(lines_ref, -1)

        @pl.loop(0, used.shape[0])
        def _(tile):
            used[tile] = 0

    in_iota = lax.broadcasted_iota(jnp.int32, (16, width), 0).astype(jnp.float32)
    out_iota = lax.broadcasted_iota(jnp.int32, (8, width), 0).astype(jnp.float32)
    band_lane = lax.broadcasted_iota(jnp.int32, (64, GROUP * 16), 1) // 16
    lane = lax.broadcasted_iota(jnp.int32, (8, half), 1)
    slot_lane = lax.broadcasted_iota(jnp.int32, (1, lines_ref.shape[2]), 1)
    slot_line = (slot_lane % 16) // 8 * TILE_ROWS + slot_lane % 8

    def table_rows(tile):
        return 0.5 * table_ref[tile, 0:1, :], table_ref[tile, 1:2, :]

    def before(i, _):
        p = step * GROUP + i
        rate, centre = table_rows(target[p])
        u = (in_iota + (row[p].astype(jnp.float32) - (3.0 + TILE_ROWS / 2))) * (1.0 / TILE_ROWS)
        cosine, sine = unit_phasor((rate * u + centre) * u)
        real = x_ref[i, 0].astype(jnp.float32)
        imag = x_ref[i, 1].astype(jnp.float32)
        lines = pl.ds(pl.multiple_of(i * 16, 16), 16)
        deramped[lines, 0:width] = (real * cosine + imag * sine).astype(jnp.bfloat16)
        deramped[lines, width : 2 * width] = (imag * cosine - real * sine).astype(jnp.bfloat16)
        taps = taps_ref[block[p]]
        band[pl.ds(pl.multiple_of(i * 64, 64), 64), :] = jnp.where(
            band_lane == i, taps, jnp.zeros_like(taps)
        )
        return 0

    lax.fori_loop(0, GROUP, before, 0, unroll=4)
    mixed[...] = jnp.dot(band[...], deramped[...], preferred_element_type=jnp.float32)

    def after(i, _):
        p = step * GROUP + i
        tile = target[p]
        shift0 = col[p] - 3
        sums = [jnp.zeros((8, half), jnp.float32) for _ in range(4)]
        for b in range(8):
            shift = shift0 + b
            turn = lax.rem(half - shift, half)
            place = lane + shift
            inside = (place >= 0) & (place < half)
            above = (shift > 0).astype(jnp.float32)
            below = (shift < 0).astype(jnp.float32)
            lines = pl.ds(pl.multiple_of(i * 64 + b * 8, 8), 8)
            for z in range(2):
                left = pltpu.roll(mixed[lines, z * width : z * width + half], turn, 1)
                right = pltpu.roll(mixed[lines, z * width + half : (z + 1) * width], turn, 1)
                sums[2 * z] = sums[2 * z] + jnp.where(inside, left, right * above)
                sums[2 * z + 1] = sums[2 * z + 1] + jnp.where(inside, right, left * below)
        real = jnp.concatenate(sums[0:2], axis=1)
        imag = jnp.concatenate(sums[2:4], axis=1)
        rate, centre = table_rows(tile)
        start = (
            row[p].astype(jnp.float32)
            + block[p].astype(jnp.float32) * (1.0 / WEIGHT_BLOCKS)
            - TILE_ROWS / 2
        )
        u = (out_iota + start) * (1.0 / TILE_ROWS)
        cosine, sine = unit_phasor((rate * u + centre) * u)
        out_real = real * cosine - imag * sine
        out_imag = imag * cosine + real * sine
        out_ref[i, 0] = out_real.astype(jnp.bfloat16)
        out_ref[i, 1] = out_imag.astype(jnp.bfloat16)
        slot = used[tile]
        used[tile] = slot + 1
        message_ref[tile, pl.ds(pl.multiple_of(slot * 16, 16), 16), :] = jnp.concatenate(
            [out_real, out_imag], axis=0
        ).astype(jnp.bfloat16)
        lines_ref[tile, 0:1, :] = jnp.where(
            slot_lane // 16 == slot, slot_line + row[p], lines_ref[tile, 0:1, :]
        )
        return 0

    lax.fori_loop(0, GROUP, after, 0, unroll=2)


def resample(pieces, target, block, row, col, tables, taps, capacity):
    count, _, in_rows, width = pieces.shape
    tiles = tables.shape[0]
    rows = capacity * 16
    lanes = max(128, rows)
    whole = lambda *shape: pl.BlockSpec(shape, lambda g, *_: (0,) * len(shape))
    return pl.pallas_call(
        functools.partial(resample_kernel, capacity),
        grid_spec=pltpu.PrefetchScalarGridSpec(
            num_scalar_prefetch=4,
            grid=(count // GROUP,),
            in_specs=[
                pl.BlockSpec((GROUP, 2, in_rows, width), lambda g, *_: (g, 0, 0, 0)),
                whole(*tables.shape),
                whole(*taps.shape),
            ],
            out_specs=[
                pl.BlockSpec((GROUP, 2, 8, width), lambda g, *_: (g, 0, 0, 0)),
                whole(tiles, rows, width),
                whole(tiles, 8, lanes),
            ],
            scratch_shapes=[
                pltpu.VMEM((GROUP * 16, 2 * width), jnp.bfloat16),
                pltpu.VMEM((GROUP * 64, GROUP * 16), jnp.bfloat16),
                pltpu.VMEM((GROUP * 64, 2 * width), jnp.float32),
                pltpu.SMEM((tiles,), jnp.int32),
            ],
        ),
        out_shape=[
            jax.ShapeDtypeStruct((count, 2, 8, width), jnp.bfloat16),
            jax.ShapeDtypeStruct((tiles, rows, width), jnp.bfloat16),
            jax.ShapeDtypeStruct((tiles, 8, lanes), jnp.int32),
        ],
        compiler_params=pltpu.CompilerParams(
            dimension_semantics=("arbitrary",), vmem_limit_bytes=40 * 1024 * 1024
        ),
        name="resample",
    )(target, block, row, col, pieces, tables, taps)


def exchange_kernel(
    n,
    length_ref,
    message_ref,
    lines_ref,
    tile_ref,
    out_ref,
    sum_ref,
    got,
    got_lines,
    total,
    tail,
    previous,
    own_sem,
    send_sem,
    recv_sem,
    lines_send_sem,
    lines_recv_sem,
    tail_sem,
):
    me = lax.axis_index("az")
    height = tile_ref.shape[1]
    rows = message_ref.shape[1]

    def own(part):
        if part:
            return pltpu.make_async_copy(lines_ref.at[me], got_lines.at[0], own_sem.at[1])
        return pltpu.make_async_copy(message_ref.at[me], got.at[0], own_sem.at[0])

    def data_copy(k):
        to = lax.rem(me + k, n)
        return pltpu.make_async_remote_copy(
            src_ref=message_ref.at[to],
            dst_ref=got.at[k],
            send_sem=send_sem.at[k],
            recv_sem=recv_sem.at[k],
            device_id={"az": to},
            device_id_type=MESH,
        )

    def lines_copy(k):
        to = lax.rem(me + k, n)
        return pltpu.make_async_remote_copy(
            src_ref=lines_ref.at[to],
            dst_ref=got_lines.at[k],
            send_sem=lines_send_sem.at[k],
            recv_sem=lines_recv_sem.at[k],
            device_id={"az": to},
            device_id_type=MESH,
        )

    own(0).start()
    own(1).start()
    barrier = pltpu.get_barrier_semaphore()

    @pl.loop(1, n)
    def _(k):
        pl.semaphore_signal(
            barrier, inc=1, device_id={"az": lax.rem(me + k, n)}, device_id_type=MESH
        )

    pl.semaphore_wait(barrier, n - 1)

    @pl.loop(1, n)
    def _(k):
        lines_copy(k).start()
        data_copy(k).start()

    wanted = lax.broadcasted_iota(jnp.int32, (2 * height, rows), 0)

    def placed(k):
        pick = (wanted == got_lines[k, 0:1, 0:rows]).astype(jnp.bfloat16)
        return jnp.dot(pick, got[k], preferred_element_type=jnp.float32)

    own(0).wait()
    own(1).wait()
    total[...] = placed(0)

    @pl.loop(1, n)
    def _(k):
        lines_copy(k).wait_recv()
        data_copy(k).wait_recv()
        total[...] += placed(k)

    ref_real, ref_imag = tile_ref[0], tile_ref[1]
    got_real, got_imag = total[0:height, :], total[height : 2 * height, :]
    out_ref[0] = ref_real * got_real + ref_imag * got_imag
    out_ref[1] = ref_imag * got_real - ref_real * got_imag
    tail[...] = out_ref[:, height - INTERSECTION : height, :]
    tail_copy = pltpu.make_async_remote_copy(
        src_ref=tail,
        dst_ref=previous,
        send_sem=tail_sem.at[0],
        recv_sem=tail_sem.at[1],
        device_id={"az": lax.rem(me + 1, n)},
        device_id_type=MESH,
    )
    tail_copy.start()
    length = length_ref[0]
    apart = lax.broadcasted_iota(
        jnp.int32, (INTERSECTION, INTERSECTION), 1
    ) - lax.broadcasted_iota(jnp.int32, (INTERSECTION, INTERSECTION), 0)
    shifter = (apart == INTERSECTION - length).astype(jnp.float32)
    tail_copy.wait_recv()
    before = [
        jnp.dot(
            shifter,
            previous[z],
            precision=lax.Precision.HIGHEST,
            preferred_element_type=jnp.float32,
        )
        for z in range(2)
    ]
    head = [out_ref[z, 0:INTERSECTION, :] for z in range(2)]
    scale = jnp.where(me == 0, 0.0, 1.0) / length.astype(jnp.float32)
    sum_ref[0, 0:1, :] = scale * jnp.sum(
        head[0] * before[0] + head[1] * before[1], axis=0, keepdims=True
    )
    sum_ref[0, 1:2, :] = scale * jnp.sum(
        head[1] * before[0] - head[0] * before[1], axis=0, keepdims=True
    )

    @pl.loop(1, n)
    def _(k):
        lines_copy(k).wait_send()
        data_copy(k).wait_send()

    tail_copy.wait_send()


def exchange(message, lines, tile, length):
    n, rows, width = message.shape
    height = tile.shape[1]
    return pl.pallas_call(
        functools.partial(exchange_kernel, n),
        in_specs=[
            pl.BlockSpec(memory_space=pltpu.SMEM),
            pl.BlockSpec(memory_space=pl.ANY),
            pl.BlockSpec(memory_space=pl.ANY),
            pl.BlockSpec(memory_space=pltpu.VMEM),
        ],
        out_specs=[pl.BlockSpec(memory_space=pltpu.VMEM)] * 2,
        out_shape=[
            jax.ShapeDtypeStruct(tile.shape, jnp.float32),
            jax.ShapeDtypeStruct((1, 2, width), jnp.float32),
        ],
        scratch_shapes=[
            pltpu.VMEM((n, rows, width), jnp.bfloat16),
            pltpu.VMEM(lines.shape, jnp.int32),
            pltpu.VMEM((2 * height, width), jnp.float32),
            pltpu.VMEM((2, INTERSECTION, width), jnp.float32),
            pltpu.VMEM((2, INTERSECTION, width), jnp.float32),
            pltpu.SemaphoreType.DMA((2,)),
            pltpu.SemaphoreType.DMA((n,)),
            pltpu.SemaphoreType.DMA((n,)),
            pltpu.SemaphoreType.DMA((n,)),
            pltpu.SemaphoreType.DMA((n,)),
            pltpu.SemaphoreType.DMA((2,)),
        ],
        compiler_params=pltpu.CompilerParams(
            collective_id=0, has_side_effects=True, vmem_limit_bytes=40 * 1024 * 1024
        ),
        name="exchange",
    )(length, message, lines, tile)


def tap_table(sinc_blocks):
    blocks = sinc_blocks.shape[0]
    a = jnp.arange(8)[:, None, None]
    r = jnp.arange(8)[None, :, None]
    q = jnp.arange(GROUP * 16)[None, None, :] % 16
    place = (q == r + a).astype(jnp.bfloat16)
    taps = jnp.einsum(
        "nab,arq->nbrq",
        sinc_blocks.astype(jnp.bfloat16),
        place,
        preferred_element_type=jnp.float32,
    ).astype(jnp.bfloat16)
    return taps.reshape(blocks, 64, GROUP * 16)


def on_device(
    secondary_pieces,
    piece_target,
    piece_block,
    piece_row,
    piece_column,
    ramp_rate,
    centroid,
    sinc_blocks,
    reference_tile,
    intersection_rows,
):
    tile_count = lax.axis_size("az")
    capacity = max(2, 2 * secondary_pieces.shape[0] // tile_count)
    tables = lax.all_gather(jnp.stack([ramp_rate, centroid], axis=1), "az", tiled=True)
    coregistered, message, lines = resample(
        secondary_pieces,
        piece_target[:, 0],
        piece_block,
        piece_row,
        piece_column,
        tables,
        tap_table(sinc_blocks),
        capacity,
    )
    interferogram, diversity = exchange(message, lines, reference_tile, intersection_rows)
    return coregistered, interferogram, diversity


def solution(mesh):
    split = ("dates", "az")
    return jax.shard_map(
        on_device,
        mesh=mesh,
        in_specs=(
            P(split, None, None, None),
            P(split, None),
            P(split),
            P(split),
            P(split),
            P(split, None),
            P(split, None),
            P(),
            P(None, split, None),
            P(split),
        ),
        out_specs=(
            P(split, None, None, None),
            P(None, split, None),
            P(split, None, None),
        ),
        check_vma=False,
    )
```

```python
import functools

import jax
import jax.numpy as jnp
from jax import lax
from jax.experimental import pallas as pl
from jax.experimental.pallas import tpu as pltpu
from jax.sharding import PartitionSpec as P

TILE_ROWS = 256
INTERSECTION = 32
WEIGHT_BLOCKS = 64
GROUP = 16
MATES = 4
MESH = pl.DeviceIdType.MESH

SIN_FIT = (6.2831807136535645, -41.33925247192383, 81.40833282470703, -71.61119079589844)
COS_FIT = (0.9999932646751404, -19.73573875427246, 64.65997314453125, -78.21002960205078)


def unit_phasor(turns):
    part = turns - jnp.round(turns)
    w = 0.25 - jnp.abs(part)
    w2 = w * w
    even = jnp.full_like(w2, COS_FIT[-1])
    for coeff in COS_FIT[-2::-1]:
        even = even * w2 + coeff
    odd = jnp.full_like(w2, SIN_FIT[-1])
    for coeff in SIN_FIT[-2::-1]:
        odd = odd * w2 + coeff
    return odd * w, jnp.where(part < 0, -even, even)


def resample_kernel(
    capacity,
    target,
    block,
    row,
    col,
    x_ref,
    table_ref,
    taps_ref,
    out_ref,
    message_ref,
    lines_ref,
    deramped,
    band,
    mixed,
    used,
):
    step = pl.program_id(0)
    width = x_ref.shape[3]
    half = width // 2

    @pl.when(step == 0)
    def _():
        message_ref[...] = jnp.zeros_like(message_ref)
        lines_ref[...] = jnp.full_like(lines_ref, -1)

        @pl.loop(0, used.shape[0])
        def _(tile):
            used[tile] = 0

    in_iota = lax.broadcasted_iota(jnp.int32, (16, width), 0).astype(jnp.float32)
    out_iota = lax.broadcasted_iota(jnp.int32, (8, width), 0).astype(jnp.float32)
    band_lane = lax.broadcasted_iota(jnp.int32, (64, GROUP * 16), 1) // 16
    lane = lax.broadcasted_iota(jnp.int32, (8, half), 1)
    slot_lane = lax.broadcasted_iota(jnp.int32, (1, lines_ref.shape[2]), 1)
    slot_line = (slot_lane % 16) // 8 * TILE_ROWS + slot_lane % 8

    def table_rows(tile):
        return 0.5 * table_ref[tile, 0:1, :], table_ref[tile, 1:2, :]

    def before(i, _):
        p = step * GROUP + i
        rate, centre = table_rows(target[p])
        u = (in_iota + (row[p].astype(jnp.float32) - (3.0 + TILE_ROWS / 2))) * (1.0 / TILE_ROWS)
        cosine, sine = unit_phasor((rate * u + centre) * u)
        real = x_ref[i, 0].astype(jnp.float32)
        imag = x_ref[i, 1].astype(jnp.float32)
        lines = pl.ds(pl.multiple_of(i * 16, 16), 16)
        deramped[lines, 0:width] = (real * cosine + imag * sine).astype(jnp.bfloat16)
        deramped[lines, width : 2 * width] = (imag * cosine - real * sine).astype(jnp.bfloat16)
        taps = taps_ref[block[p]]
        band[pl.ds(pl.multiple_of(i * 64, 64), 64), :] = jnp.where(
            band_lane == i, taps, jnp.zeros_like(taps)
        )
        return 0

    lax.fori_loop(0, GROUP, before, 0, unroll=4)
    mixed[...] = jnp.dot(band[...], deramped[...], preferred_element_type=jnp.float32)

    def after(i, _):
        p = step * GROUP + i
        tile = target[p]
        shift0 = col[p] - 3
        sums = [jnp.zeros((8, half), jnp.float32) for _ in range(4)]
        for b in range(8):
            shift = shift0 + b
            turn = lax.rem(half - shift, half)
            place = lane + shift
            inside = (place >= 0) & (place < half)
            above = (shift > 0).astype(jnp.float32)
            below = (shift < 0).astype(jnp.float32)
            lines = pl.ds(pl.multiple_of(i * 64 + b * 8, 8), 8)
            for z in range(2):
                left = pltpu.roll(mixed[lines, z * width : z * width + half], turn, 1)
                right = pltpu.roll(mixed[lines, z * width + half : (z + 1) * width], turn, 1)
                sums[2 * z] = sums[2 * z] + jnp.where(inside, left, right * above)
                sums[2 * z + 1] = sums[2 * z + 1] + jnp.where(inside, right, left * below)
        real = jnp.concatenate(sums[0:2], axis=1)
        imag = jnp.concatenate(sums[2:4], axis=1)
        rate, centre = table_rows(tile)
        start = (
            row[p].astype(jnp.float32)
            + block[p].astype(jnp.float32) * (1.0 / WEIGHT_BLOCKS)
            - TILE_ROWS / 2
        )
        u = (out_iota + start) * (1.0 / TILE_ROWS)
        cosine, sine = unit_phasor((rate * u + centre) * u)
        out_real = real * cosine - imag * sine
        out_imag = imag * cosine + real * sine
        out_ref[i, 0] = out_real.astype(jnp.bfloat16)
        out_ref[i, 1] = out_imag.astype(jnp.bfloat16)
        slot = used[tile]
        used[tile] = slot + 1
        message_ref[tile, pl.ds(pl.multiple_of(slot * 16, 16), 16), :] = jnp.concatenate(
            [out_real, out_imag], axis=0
        ).astype(jnp.bfloat16)
        mate, plane = lax.rem(tile, MATES), pl.ds(tile // MATES, 1)
        lines_ref[mate, plane, :] = jnp.where(
            slot_lane // 16 == slot, slot_line + row[p], lines_ref[mate, plane, :]
        )
        return 0

    lax.fori_loop(0, GROUP, after, 0, unroll=2)


def resample(pieces, target, block, row, col, tables, taps, capacity):
    count, _, in_rows, width = pieces.shape
    tiles = tables.shape[0]
    rows = capacity * 16
    line_shape = (MATES, max(8, tiles // MATES), max(128, rows))
    whole = lambda *shape: pl.BlockSpec(shape, lambda g, *_: (0,) * len(shape))
    return pl.pallas_call(
        functools.partial(resample_kernel, capacity),
        grid_spec=pltpu.PrefetchScalarGridSpec(
            num_scalar_prefetch=4,
            grid=(count // GROUP,),
            in_specs=[
                pl.BlockSpec((GROUP, 2, in_rows, width), lambda g, *_: (g, 0, 0, 0)),
                whole(*tables.shape),
                whole(*taps.shape),
            ],
            out_specs=[
                pl.BlockSpec((GROUP, 2, 8, width), lambda g, *_: (g, 0, 0, 0)),
                whole(tiles, rows, width),
                whole(*line_shape),
            ],
            scratch_shapes=[
                pltpu.VMEM((GROUP * 16, 2 * width), jnp.bfloat16),
                pltpu.VMEM((GROUP * 64, GROUP * 16), jnp.bfloat16),
                pltpu.VMEM((GROUP * 64, 2 * width), jnp.float32),
                pltpu.SMEM((tiles,), jnp.int32),
            ],
        ),
        out_shape=[
            jax.ShapeDtypeStruct((count, 2, 8, width), jnp.bfloat16),
            jax.ShapeDtypeStruct((tiles, rows, width), jnp.bfloat16),
            jax.ShapeDtypeStruct(line_shape, jnp.int32),
        ],
        compiler_params=pltpu.CompilerParams(
            dimension_semantics=("arbitrary",), vmem_limit_bytes=40 * 1024 * 1024
        ),
        name="resample",
    )(target, block, row, col, pieces, tables, taps)


def gather_kernel(n, rate_ref, centre_ref, sinc_ref, out_ref, taps_ref, own, got, wide, send_sem, recv_sem):
    me = lax.axis_index("az")
    barrier = pltpu.get_barrier_semaphore()

    def to_all(k):
        to = lax.rem(me + k, n)
        return pltpu.make_async_remote_copy(
            src_ref=own,
            dst_ref=got.at[me],
            send_sem=send_sem.at[k],
            recv_sem=recv_sem.at[k],
            device_id={"az": to},
            device_id_type=MESH,
        )

    def from_all(k):
        return pltpu.make_async_remote_copy(
            src_ref=own,
            dst_ref=got.at[lax.rem(me - k + n, n)],
            send_sem=send_sem.at[k],
            recv_sem=recv_sem.at[k],
            device_id={"az": lax.rem(me + k, n)},
            device_id_type=MESH,
        )

    @pl.loop(1, n)
    def _(k):
        pl.semaphore_signal(
            barrier, inc=1, device_id={"az": lax.rem(me + k, n)}, device_id_type=MESH
        )

    own[0:1, :] = rate_ref[...]
    own[1:2, :] = centre_ref[...]
    got[me] = own[...]
    pl.semaphore_wait(barrier, n - 1)

    @pl.loop(1, n)
    def _(k):
        to_all(k).start()

    blocks = sinc_ref.shape[2]
    place = (
        lax.broadcasted_iota(jnp.int32, (8, 128), 1) % 16
        == lax.broadcasted_iota(jnp.int32, (8, 128), 0)
    ).astype(jnp.float32)
    for b in range(8):
        wide[b] = lax.dot_general(
            sinc_ref[b],
            place,
            (((0,), (0,)), ((), ())),
            preferred_element_type=jnp.float32,
        )

    @pl.loop(0, blocks)
    def _(block):
        for b in range(0, 8, 2):
            pair = jnp.concatenate(
                [
                    pltpu.roll(
                        jnp.broadcast_to(wide[b + e, pl.ds(block, 1), :], (8, 128)),
                        0,
                        1,
                        stride=1,
                        stride_axis=0,
                    )
                    for e in range(2)
                ],
                axis=0,
            ).astype(jnp.bfloat16)
            for half in range(0, GROUP * 16, 128):
                taps_ref[block, b * 8 : b * 8 + 16, half : half + 128] = pair

    @pl.loop(1, n)
    def _(k):
        from_all(k).wait_recv()

    out_ref[...] = got[...]

    @pl.loop(1, n)
    def _(k):
        to_all(k).wait_send()


def gather_tables(rate, centre, sinc_blocks):
    n = lax.axis_size("az")
    width = rate.shape[1]
    blocks = sinc_blocks.shape[0]
    return pl.pallas_call(
        functools.partial(gather_kernel, n),
        in_specs=[pl.BlockSpec(memory_space=pltpu.VMEM)] * 3,
        out_specs=[pl.BlockSpec(memory_space=pltpu.VMEM)] * 2,
        out_shape=[
            jax.ShapeDtypeStruct((n, 2, width), jnp.float32),
            jax.ShapeDtypeStruct((blocks, 64, GROUP * 16), jnp.bfloat16),
        ],
        scratch_shapes=[
            pltpu.VMEM((2, width), jnp.float32),
            pltpu.VMEM((n, 2, width), jnp.float32),
            pltpu.VMEM((8, blocks, 128), jnp.float32),
            pltpu.SemaphoreType.DMA((n,)),
            pltpu.SemaphoreType.DMA((n,)),
        ],
        compiler_params=pltpu.CompilerParams(
            collective_id=1, has_side_effects=True, vmem_limit_bytes=32 * 1024 * 1024
        ),
        name="gather_tables",
    )(rate, centre, jnp.transpose(sinc_blocks, (2, 1, 0)))


def exchange_kernel(
    n,
    length_ref,
    message_ref,
    lines_ref,
    tile_ref,
    out_ref,
    sum_ref,
    got,
    got_lines,
    part,
    got_part,
    total,
    tail,
    previous,
    send_sem,
    recv_sem,
    lines_send_sem,
    lines_recv_sem,
    part_send_sem,
    part_recv_sem,
    tail_sem,
):
    me = lax.axis_index("az")
    height = tile_ref.shape[1]
    rows = message_ref.shape[1]
    m = n // MATES
    high, low = me // MATES, lax.rem(me, MATES)

    def mate(e):
        return high * MATES + lax.rem(low + e, MATES)

    def peer(k):
        return lax.rem(high + k, m) * MATES + low

    def lines_copy(e):
        return pltpu.make_async_remote_copy(
            src_ref=lines_ref.at[lax.rem(low + e, MATES)],
            dst_ref=got_lines.at[e],
            send_sem=lines_send_sem.at[e],
            recv_sem=lines_recv_sem.at[e],
            device_id={"az": mate(e)},
            device_id_type=MESH,
        )

    def data_copy(k, e):
        tile = lax.rem(high + k, m) * MATES + lax.rem(low + e, MATES)
        return pltpu.make_async_remote_copy(
            src_ref=message_ref.at[tile],
            dst_ref=got.at[k, e],
            send_sem=send_sem.at[k, e],
            recv_sem=recv_sem.at[k, e],
            device_id={"az": mate(e)},
            device_id_type=MESH,
        )

    def part_copy(k):
        return pltpu.make_async_remote_copy(
            src_ref=part.at[k],
            dst_ref=got_part.at[k],
            send_sem=part_send_sem.at[k],
            recv_sem=part_recv_sem.at[k],
            device_id={"az": peer(k)},
            device_id_type=MESH,
        )

    tail_copy = pltpu.make_async_remote_copy(
        src_ref=tail,
        dst_ref=previous,
        send_sem=tail_sem.at[0],
        recv_sem=tail_sem.at[1],
        device_id={"az": lax.rem(me + 1, n)},
        device_id_type=MESH,
    )

    barrier = pltpu.get_barrier_semaphore()
    for e in range(1, MATES):
        pl.semaphore_signal(barrier, inc=1, device_id={"az": mate(e)}, device_id_type=MESH)

    @pl.loop(1, m)
    def _(k):
        pl.semaphore_signal(barrier, inc=1, device_id={"az": peer(k)}, device_id_type=MESH)

    @pl.when(low == 0)
    def _():
        pl.semaphore_signal(
            barrier, inc=1, device_id={"az": lax.rem(me + n - 1, n)}, device_id_type=MESH
        )

    @pl.when(me == 0)
    def _():
        previous[...] = jnp.zeros_like(previous)

    pl.semaphore_wait(barrier, MATES - 1 + m - 1 + low // (MATES - 1))

    for e in range(1, MATES):
        lines_copy(e).start()

    def order(j):
        return 1 + lax.rem(j + m // 2 - 1, m - 1) if m > 1 else 0

    @pl.loop(0, m - 1)
    def _(j):
        for e in range(1, MATES):
            data_copy(order(j), e).start()

    for e in range(1, MATES):
        data_copy(0, e).start()

    wanted = lax.broadcasted_iota(jnp.int32, (2 * height, rows), 0)

    def placed(lines, data):
        pick = (wanted == lines).astype(jnp.bfloat16)
        return jnp.dot(pick, data, preferred_element_type=jnp.float32)

    def summed(k):
        plane = lax.rem(high + k, m)
        result = placed(lines_ref[low, pl.ds(plane, 1), 0:rows], message_ref[peer(k)])
        for e in range(1, MATES):
            data_copy(k, e).wait_recv()
            result = result + placed(got_lines[e, pl.ds(plane, 1), 0:rows], got[k, e])
        return result

    for e in range(1, MATES):
        lines_copy(e).wait_recv()

    @pl.loop(0, m - 1)
    def _(j):
        k = order(j)
        part[k] = summed(k).astype(jnp.bfloat16)
        part_copy(k).start()

    total[...] = summed(0)

    @pl.loop(0, m - 1)
    def _(j):
        k = order(j)
        part_copy(k).wait_recv()
        total[...] += got_part[k].astype(jnp.float32)

    ref_real, ref_imag = tile_ref[0], tile_ref[1]
    got_real, got_imag = total[0:height, :], total[height : 2 * height, :]
    out_ref[0] = ref_real * got_real + ref_imag * got_imag
    out_ref[1] = ref_imag * got_real - ref_real * got_imag
    tail[...] = out_ref[:, height - INTERSECTION : height, :]

    @pl.when(me < n - 1)
    def _():
        tail_copy.start()

    length = length_ref[0]
    apart = lax.broadcasted_iota(
        jnp.int32, (INTERSECTION, INTERSECTION), 1
    ) - lax.broadcasted_iota(jnp.int32, (INTERSECTION, INTERSECTION), 0)
    shifter = (apart == INTERSECTION - length).astype(jnp.float32)

    @pl.when(me > 0)
    def _():
        tail_copy.wait_recv()

    before = [
        jnp.dot(
            shifter,
            previous[z],
            precision=lax.Precision.HIGHEST,
            preferred_element_type=jnp.float32,
        )
        for z in range(2)
    ]
    head = [out_ref[z, 0:INTERSECTION, :] for z in range(2)]
    scale = 1.0 / length.astype(jnp.float32)
    sum_ref[0, 0:1, :] = scale * jnp.sum(
        head[0] * before[0] + head[1] * before[1], axis=0, keepdims=True
    )
    sum_ref[0, 1:2, :] = scale * jnp.sum(
        head[1] * before[0] - head[0] * before[1], axis=0, keepdims=True
    )

    for e in range(1, MATES):
        lines_copy(e).wait_send()

    @pl.loop(0, m)
    def _(k):
        for e in range(1, MATES):
            data_copy(k, e).wait_send()

    @pl.loop(1, m)
    def _(k):
        part_copy(k).wait_send()

    @pl.when(me < n - 1)
    def _():
        tail_copy.wait_send()


def exchange(message, lines, tile, length):
    n, rows, width = message.shape
    height = tile.shape[1]
    m = n // MATES
    dma = pltpu.SemaphoreType.DMA
    return pl.pallas_call(
        functools.partial(exchange_kernel, n),
        in_specs=[pl.BlockSpec(memory_space=pltpu.SMEM)]
        + [pl.BlockSpec(memory_space=pltpu.VMEM)] * 3,
        out_specs=[pl.BlockSpec(memory_space=pltpu.VMEM)] * 2,
        out_shape=[
            jax.ShapeDtypeStruct(tile.shape, jnp.float32),
            jax.ShapeDtypeStruct((1, 2, width), jnp.float32),
        ],
        scratch_shapes=[
            pltpu.VMEM((m, MATES, rows, width), jnp.bfloat16),
            pltpu.VMEM(lines.shape, jnp.int32),
            pltpu.VMEM((m, 2 * height, width), jnp.bfloat16),
            pltpu.VMEM((m, 2 * height, width), jnp.bfloat16),
            pltpu.VMEM((2 * height, width), jnp.float32),
            pltpu.VMEM((2, INTERSECTION, width), jnp.float32),
            pltpu.VMEM((2, INTERSECTION, width), jnp.float32),
            dma((m, MATES)),
            dma((m, MATES)),
            dma((MATES,)),
            dma((MATES,)),
            dma((m,)),
            dma((m,)),
            dma((2,)),
        ],
        compiler_params=pltpu.CompilerParams(
            collective_id=0, has_side_effects=True, vmem_limit_bytes=48 * 1024 * 1024
        ),
        name="exchange",
    )(length, message, lines, tile)


def on_device(
    secondary_pieces,
    piece_target,
    piece_block,
    piece_row,
    piece_column,
    ramp_rate,
    centroid,
    sinc_blocks,
    reference_tile,
    intersection_rows,
):
    tile_count = lax.axis_size("az")
    capacity = max(2, 2 * secondary_pieces.shape[0] // tile_count)
    tables, taps = gather_tables(ramp_rate, centroid, sinc_blocks)
    coregistered, message, lines = resample(
        secondary_pieces,
        piece_target[:, 0],
        piece_block,
        piece_row,
        piece_column,
        tables,
        taps,
        capacity,
    )
    interferogram, diversity = exchange(message, lines, reference_tile, intersection_rows)
    return coregistered, interferogram, diversity


def solution(mesh):
    split = ("dates", "az")
    return jax.shard_map(
        on_device,
        mesh=mesh,
        in_specs=(
            P(split, None, None, None),
            P(split, None),
            P(split),
            P(split),
            P(split),
            P(split, None),
            P(split, None),
            P(),
            P(None, split, None),
            P(split),
        ),
        out_specs=(
            P(split, None, None, None),
            P(None, split, None),
            P(split, None, None),
        ),
        check_vma=False,
    )
```

```python
import functools

import jax
import jax.numpy as jnp
from jax import lax
from jax.experimental import pallas as pl
from jax.experimental.pallas import tpu as pltpu
from jax.sharding import PartitionSpec as P

TILE_ROWS = 256
INTERSECTION = 32
WEIGHT_BLOCKS = 64
GROUP = 16
MATES = 8
VMEM_BYTES = 63 * 1024 * 1024
MESH = pl.DeviceIdType.MESH

SIN_FIT = (6.2831807136535645, -41.33925247192383, 81.40833282470703, -71.61119079589844)
COS_FIT = (0.9999932646751404, -19.73573875427246, 64.65997314453125, -78.21002960205078)


def unit_phasor(turns):
    part = turns - jnp.round(turns)
    w = 0.25 - jnp.abs(part)
    w2 = w * w
    even = jnp.full_like(w2, COS_FIT[-1])
    for coeff in COS_FIT[-2::-1]:
        even = even * w2 + coeff
    odd = jnp.full_like(w2, SIN_FIT[-1])
    for coeff in SIN_FIT[-2::-1]:
        odd = odd * w2 + coeff
    return odd * w, jnp.where(part < 0, -even, even)


def resample_kernel(
    target_ref,
    block_ref,
    row_ref,
    col_ref,
    pieces_ref,
    table_ref,
    taps_hbm,
    out_ref,
    message_ref,
    lines_ref,
    deramped,
    band,
    mixed,
    used,
    target,
    block,
    row,
    col,
    pieces,
    taps_ref,
    fetch_sem,
    pieces_sem,
):
    step = pl.program_id(0)
    width = pieces_ref.shape[3]
    half = width // 2
    fetches = [
        pltpu.make_async_copy(source, scalars, fetch_sem.at[i])
        for i, (source, scalars) in enumerate(
            [
                (target_ref, target),
                (block_ref, block),
                (row_ref, row),
                (col_ref, col),
                (taps_hbm, taps_ref),
            ]
        )
    ]

    def pieces_copy(group):
        part = pl.ds(group * GROUP, GROUP)
        return pltpu.make_async_copy(
            pieces_ref.at[part], pieces.at[part], pieces_sem.at[group]
        )

    @pl.when(step == 0)
    def _():
        for fetch in fetches:
            fetch.start()

        @pl.loop(0, pieces_ref.shape[0] // GROUP)
        def _(group):
            pieces_copy(group).start()

        message_ref[...] = jnp.zeros_like(message_ref)
        lines_ref[...] = jnp.full_like(lines_ref, -1)

        @pl.loop(0, used.shape[0])
        def _(tile):
            used[tile] = 0

        for fetch in fetches:
            fetch.wait()

    pieces_copy(step).wait()

    in_iota = lax.broadcasted_iota(jnp.int32, (16, width), 0).astype(jnp.float32)
    out_iota = lax.broadcasted_iota(jnp.int32, (8, width), 0).astype(jnp.float32)
    band_lane = lax.broadcasted_iota(jnp.int32, (64, GROUP * 16), 1) // 16
    lane = lax.broadcasted_iota(jnp.int32, (8, half), 1)
    slot_lane = lax.broadcasted_iota(jnp.int32, (1, lines_ref.shape[2]), 1)
    slot_line = (slot_lane % 16) // 8 * TILE_ROWS + slot_lane % 8

    def table_rows(tile):
        return 0.5 * table_ref[tile, 0], table_ref[tile, 1]

    def before(i, _):
        p = step * GROUP + i
        rate, centre = table_rows(target[p])
        u = (in_iota + (row[p].astype(jnp.float32) - (3.0 + TILE_ROWS / 2))) * (1.0 / TILE_ROWS)
        cosine, sine = unit_phasor((rate * u + centre) * u)
        real = pieces[p, 0].astype(jnp.float32)
        imag = pieces[p, 1].astype(jnp.float32)
        lines = pl.ds(pl.multiple_of(i * 16, 16), 16)
        deramped[lines, 0:width] = (real * cosine + imag * sine).astype(jnp.bfloat16)
        deramped[lines, width : 2 * width] = (imag * cosine - real * sine).astype(jnp.bfloat16)
        taps = taps_ref[block[p]]
        band[pl.ds(pl.multiple_of(i * 64, 64), 64), :] = jnp.where(
            band_lane == i, taps, jnp.zeros_like(taps)
        )
        return 0

    lax.fori_loop(0, GROUP, before, 0, unroll=4)
    mixed[...] = jnp.dot(band[...], deramped[...], preferred_element_type=jnp.float32)

    def after(i, _):
        p = step * GROUP + i
        tile = target[p]
        shift0 = col[p] - 3
        sums = [jnp.zeros((8, half), jnp.float32) for _ in range(4)]
        for b in range(8):
            shift = shift0 + b
            turn = lax.rem(half - shift, half)
            place = lane + shift
            inside = (place >= 0) & (place < half)
            above = (shift > 0).astype(jnp.float32)
            below = (shift < 0).astype(jnp.float32)
            lines = pl.ds(pl.multiple_of(i * 64 + b * 8, 8), 8)
            for z in range(2):
                left = pltpu.roll(mixed[lines, z * width : z * width + half], turn, 1)
                right = pltpu.roll(mixed[lines, z * width + half : (z + 1) * width], turn, 1)
                sums[2 * z] = sums[2 * z] + jnp.where(inside, left, right * above)
                sums[2 * z + 1] = sums[2 * z + 1] + jnp.where(inside, right, left * below)
        real = jnp.concatenate(sums[0:2], axis=1)
        imag = jnp.concatenate(sums[2:4], axis=1)
        rate, centre = table_rows(tile)
        start = (
            row[p].astype(jnp.float32)
            + block[p].astype(jnp.float32) * (1.0 / WEIGHT_BLOCKS)
            - TILE_ROWS / 2
        )
        u = (out_iota + start) * (1.0 / TILE_ROWS)
        cosine, sine = unit_phasor((rate * u + centre) * u)
        out_real = real * cosine - imag * sine
        out_imag = imag * cosine + real * sine
        out_ref[i, 0] = out_real.astype(jnp.bfloat16)
        out_ref[i, 1] = out_imag.astype(jnp.bfloat16)
        slot = used[tile]
        used[tile] = slot + 1
        message_ref[tile, pl.ds(pl.multiple_of(slot * 16, 16), 16), :] = jnp.concatenate(
            [out_real, out_imag], axis=0
        ).astype(jnp.bfloat16)
        mate, plane = lax.rem(tile, MATES), pl.ds(tile // MATES, 1)
        lines_ref[mate, plane, :] = jnp.where(
            slot_lane // 16 == slot, slot_line + row[p], lines_ref[mate, plane, :]
        )
        return 0

    lax.fori_loop(0, GROUP, after, 0, unroll=2)


def resample(pieces, target, block, row, col, tables, taps, capacity):
    count, _, _, width = pieces.shape
    tiles = tables.shape[0]
    rows = capacity * 16
    line_shape = (MATES, max(8, tiles // MATES), max(128, rows))
    whole = lambda *shape: pl.BlockSpec(shape, lambda g: (0,) * len(shape))
    remote = pl.BlockSpec(memory_space=pltpu.HBM)
    return pl.pallas_call(
        resample_kernel,
        grid_spec=pltpu.PrefetchScalarGridSpec(
            num_scalar_prefetch=0,
            grid=(count // GROUP,),
            in_specs=[
                *[remote] * 5,
                whole(*tables.shape),
                remote,
            ],
            out_specs=[
                pl.BlockSpec((GROUP, 2, 8, width), lambda g: (g, 0, 0, 0)),
                whole(tiles, rows, width),
                whole(*line_shape),
            ],
            scratch_shapes=[
                pltpu.VMEM((GROUP * 16, 2 * width), jnp.bfloat16),
                pltpu.VMEM((GROUP * 64, GROUP * 16), jnp.bfloat16),
                pltpu.VMEM((GROUP * 64, 2 * width), jnp.float32),
                pltpu.SMEM((tiles,), jnp.int32),
                *[pltpu.SMEM((count,), jnp.int32)] * 4,
                pltpu.VMEM(pieces.shape, jnp.bfloat16),
                pltpu.VMEM(taps.shape, jnp.bfloat16),
                pltpu.SemaphoreType.DMA((5,)),
                pltpu.SemaphoreType.DMA((count // GROUP,)),
            ],
        ),
        out_shape=[
            jax.ShapeDtypeStruct((count, 2, 8, width), jnp.bfloat16),
            jax.ShapeDtypeStruct((tiles, rows, width), jnp.bfloat16),
            jax.ShapeDtypeStruct(line_shape, jnp.int32),
        ],
        compiler_params=pltpu.CompilerParams(
            dimension_semantics=("arbitrary",), vmem_limit_bytes=VMEM_BYTES
        ),
        name="resample",
    )(target, block, row, col, pieces, tables, taps)


def gather_kernel(
    n,
    rate_ref,
    centre_ref,
    sinc_ref,
    out_ref,
    taps_ref,
    own,
    got,
    sinc,
    wide,
    fetch_sem,
    send_sem,
    recv_sem,
):
    me = lax.axis_index("az")
    fetches = [
        pltpu.make_async_copy(rate_ref, own.at[0], fetch_sem.at[0]),
        pltpu.make_async_copy(centre_ref, own.at[1], fetch_sem.at[1]),
        pltpu.make_async_copy(sinc_ref, sinc, fetch_sem.at[2]),
    ]
    for fetch in fetches:
        fetch.start()
    barrier = pltpu.get_barrier_semaphore()

    def to_all(k):
        to = lax.rem(me + k, n)
        return pltpu.make_async_remote_copy(
            src_ref=own,
            dst_ref=got.at[me],
            send_sem=send_sem.at[k],
            recv_sem=recv_sem.at[k],
            device_id={"az": to},
            device_id_type=MESH,
        )

    def from_all(k):
        return pltpu.make_async_remote_copy(
            src_ref=own,
            dst_ref=got.at[lax.rem(me - k + n, n)],
            send_sem=send_sem.at[k],
            recv_sem=recv_sem.at[k],
            device_id={"az": lax.rem(me + k, n)},
            device_id_type=MESH,
        )

    @pl.loop(1, n)
    def _(k):
        pl.semaphore_signal(
            barrier, inc=1, device_id={"az": lax.rem(me + k, n)}, device_id_type=MESH
        )

    fetches[0].wait()
    fetches[1].wait()
    got[me] = own[...]
    pl.semaphore_wait(barrier, n - 1)

    @pl.loop(1, n)
    def _(k):
        to_all(k).start()

    fetches[2].wait()
    blocks = sinc_ref.shape[2]
    place = (
        lax.broadcasted_iota(jnp.int32, (8, 128), 1) % 16
        == lax.broadcasted_iota(jnp.int32, (8, 128), 0)
    ).astype(jnp.float32)
    for b in range(8):
        wide[b] = lax.dot_general(
            sinc[:, b, :],
            place,
            (((0,), (0,)), ((), ())),
            preferred_element_type=jnp.float32,
        )

    @pl.loop(0, blocks)
    def _(block):
        for b in range(0, 8, 2):
            pair = jnp.concatenate(
                [
                    pltpu.roll(
                        jnp.broadcast_to(wide[b + e, pl.ds(block, 1), :], (8, 128)),
                        0,
                        1,
                        stride=1,
                        stride_axis=0,
                    )
                    for e in range(2)
                ],
                axis=0,
            ).astype(jnp.bfloat16)
            for half in range(0, GROUP * 16, 128):
                taps_ref[block, b * 8 : b * 8 + 16, half : half + 128] = pair

    @pl.loop(1, n)
    def _(k):
        from_all(k).wait_recv()

    out_ref[...] = got[...]

    @pl.loop(1, n)
    def _(k):
        to_all(k).wait_send()


def gather_tables(rate, centre, sinc_blocks):
    n = lax.axis_size("az")
    width = rate.shape[1]
    blocks = sinc_blocks.shape[0]
    return pl.pallas_call(
        functools.partial(gather_kernel, n),
        in_specs=[pl.BlockSpec(memory_space=pltpu.HBM)] * 3,
        out_specs=[pl.BlockSpec(memory_space=pltpu.VMEM)] * 2,
        out_shape=[
            jax.ShapeDtypeStruct((n, 2, 1, width), jnp.float32),
            jax.ShapeDtypeStruct((blocks, 64, GROUP * 16), jnp.bfloat16),
        ],
        scratch_shapes=[
            pltpu.VMEM((2, 1, width), jnp.float32),
            pltpu.VMEM((n, 2, 1, width), jnp.float32),
            pltpu.VMEM((8, 8, blocks), jnp.float32),
            pltpu.VMEM((8, blocks, 128), jnp.float32),
            pltpu.SemaphoreType.DMA((3,)),
            pltpu.SemaphoreType.DMA((n,)),
            pltpu.SemaphoreType.DMA((n,)),
        ],
        compiler_params=pltpu.CompilerParams(
            collective_id=1, has_side_effects=True, vmem_limit_bytes=VMEM_BYTES
        ),
        name="gather_tables",
    )(rate, centre, jnp.transpose(sinc_blocks, (1, 2, 0)))


def exchange_kernel(
    n,
    length_ref,
    message_ref,
    lines_hbm,
    tile_hbm,
    out_ref,
    sum_ref,
    lines_ref,
    tile_ref,
    own_sem,
    got,
    got_lines,
    part,
    got_part,
    total,
    tail,
    previous,
    send_sem,
    recv_sem,
    lines_send_sem,
    lines_recv_sem,
    part_send_sem,
    part_recv_sem,
    tail_sem,
):
    me = lax.axis_index("az")
    height = tile_hbm.shape[1]
    rows = message_ref.shape[1]
    m = n // MATES
    lines_fetch = pltpu.make_async_copy(lines_hbm, lines_ref, own_sem.at[0])
    tile_fetch = pltpu.make_async_copy(tile_hbm, tile_ref, own_sem.at[1])
    lines_fetch.start()
    tile_fetch.start()
    high, low = me // MATES, lax.rem(me, MATES)

    def mate(e):
        return high * MATES + lax.rem(low + e, MATES)

    def peer(k):
        return lax.rem(high + k, m) * MATES + low

    def lines_copy(e):
        return pltpu.make_async_remote_copy(
            src_ref=lines_ref.at[lax.rem(low + e, MATES)],
            dst_ref=got_lines.at[e],
            send_sem=lines_send_sem.at[e],
            recv_sem=lines_recv_sem.at[e],
            device_id={"az": mate(e)},
            device_id_type=MESH,
        )

    def data_copy(k, e):
        tile = lax.rem(high + k, m) * MATES + lax.rem(low + e, MATES)
        return pltpu.make_async_remote_copy(
            src_ref=message_ref.at[tile],
            dst_ref=got.at[k, e],
            send_sem=send_sem.at[k, e],
            recv_sem=recv_sem.at[k, e],
            device_id={"az": mate(e)},
            device_id_type=MESH,
        )

    def own_copy(k):
        return pltpu.make_async_copy(message_ref.at[peer(k)], got.at[k, 0], own_sem.at[2 + k])

    def part_copy(k):
        return pltpu.make_async_remote_copy(
            src_ref=part.at[k],
            dst_ref=got_part.at[k],
            send_sem=part_send_sem.at[k],
            recv_sem=part_recv_sem.at[k],
            device_id={"az": peer(k)},
            device_id_type=MESH,
        )

    tail_copy = pltpu.make_async_remote_copy(
        src_ref=tail,
        dst_ref=previous,
        send_sem=tail_sem.at[0],
        recv_sem=tail_sem.at[1],
        device_id={"az": lax.rem(me + 1, n)},
        device_id_type=MESH,
    )

    @pl.loop(0, m)
    def _(k):
        own_copy(k).start()

    barrier = pltpu.get_barrier_semaphore()
    for e in range(1, MATES):
        pl.semaphore_signal(barrier, inc=1, device_id={"az": mate(e)}, device_id_type=MESH)

    @pl.loop(1, m)
    def _(k):
        pl.semaphore_signal(barrier, inc=1, device_id={"az": peer(k)}, device_id_type=MESH)

    @pl.when(low == 0)
    def _():
        pl.semaphore_signal(
            barrier, inc=1, device_id={"az": lax.rem(me + n - 1, n)}, device_id_type=MESH
        )

    @pl.when(me == 0)
    def _():
        previous[...] = jnp.zeros_like(previous)

    pl.semaphore_wait(barrier, MATES - 1 + m - 1 + low // (MATES - 1))

    lines_fetch.wait()
    for e in range(1, MATES):
        lines_copy(e).start()

    def order(j):
        return 1 + lax.rem(j + m // 2 - 1, m - 1) if m > 1 else 0

    @pl.loop(0, m - 1)
    def _(j):
        for e in range(1, MATES):
            data_copy(order(j), e).start()

    for e in range(1, MATES):
        data_copy(0, e).start()

    wanted = lax.broadcasted_iota(jnp.int32, (2 * height, rows), 0)

    def placed(lines, data):
        pick = (wanted == lines).astype(jnp.bfloat16)
        return jnp.dot(pick, data, preferred_element_type=jnp.float32)

    def summed(k):
        plane = lax.rem(high + k, m)
        own_copy(k).wait()
        result = placed(lines_ref[low, pl.ds(plane, 1), 0:rows], got[k, 0])
        for e in range(1, MATES):
            data_copy(k, e).wait_recv()
            result = result + placed(got_lines[e, pl.ds(plane, 1), 0:rows], got[k, e])
        return result

    for e in range(1, MATES):
        lines_copy(e).wait_recv()

    @pl.loop(0, m - 1)
    def _(j):
        k = order(j)
        part[k] = summed(k).astype(jnp.bfloat16)
        part_copy(k).start()

    total[...] = summed(0)

    @pl.loop(0, m - 1)
    def _(j):
        k = order(j)
        part_copy(k).wait_recv()
        total[...] += got_part[k].astype(jnp.float32)

    tile_fetch.wait()
    ref_real, ref_imag = tile_ref[0], tile_ref[1]
    got_real, got_imag = total[0:height, :], total[height : 2 * height, :]
    out_ref[0] = ref_real * got_real + ref_imag * got_imag
    out_ref[1] = ref_imag * got_real - ref_real * got_imag
    tail[...] = out_ref[:, height - INTERSECTION : height, :]

    @pl.when(me < n - 1)
    def _():
        tail_copy.start()

    length = length_ref[0]
    apart = lax.broadcasted_iota(
        jnp.int32, (INTERSECTION, INTERSECTION), 1
    ) - lax.broadcasted_iota(jnp.int32, (INTERSECTION, INTERSECTION), 0)
    shifter = (apart == INTERSECTION - length).astype(jnp.float32)

    @pl.when(me > 0)
    def _():
        tail_copy.wait_recv()

    before = [
        jnp.dot(
            shifter,
            previous[z],
            precision=lax.Precision.HIGHEST,
            preferred_element_type=jnp.float32,
        )
        for z in range(2)
    ]
    head = [out_ref[z, 0:INTERSECTION, :] for z in range(2)]
    scale = 1.0 / length.astype(jnp.float32)
    sum_ref[0, 0:1, :] = scale * jnp.sum(
        head[0] * before[0] + head[1] * before[1], axis=0, keepdims=True
    )
    sum_ref[0, 1:2, :] = scale * jnp.sum(
        head[1] * before[0] - head[0] * before[1], axis=0, keepdims=True
    )

    for e in range(1, MATES):
        lines_copy(e).wait_send()

    @pl.loop(0, m)
    def _(k):
        for e in range(1, MATES):
            data_copy(k, e).wait_send()

    @pl.loop(1, m)
    def _(k):
        part_copy(k).wait_send()

    @pl.when(me < n - 1)
    def _():
        tail_copy.wait_send()


def exchange(message, lines, tile, length):
    n, rows, width = message.shape
    height = tile.shape[1]
    m = n // MATES
    dma = pltpu.SemaphoreType.DMA
    return pl.pallas_call(
        functools.partial(exchange_kernel, n),
        in_specs=[pl.BlockSpec(memory_space=pltpu.SMEM)]
        + [pl.BlockSpec(memory_space=pltpu.HBM)] * 3,
        out_specs=[pl.BlockSpec(memory_space=pltpu.VMEM)] * 2,
        out_shape=[
            jax.ShapeDtypeStruct(tile.shape, jnp.float32),
            jax.ShapeDtypeStruct((1, 2, width), jnp.float32),
        ],
        scratch_shapes=[
            pltpu.VMEM(lines.shape, jnp.int32),
            pltpu.VMEM(tile.shape, jnp.float32),
            dma((2 + m,)),
            pltpu.VMEM((m, MATES, rows, width), jnp.bfloat16),
            pltpu.VMEM(lines.shape, jnp.int32),
            pltpu.VMEM((m, 2 * height, width), jnp.bfloat16),
            pltpu.VMEM((m, 2 * height, width), jnp.bfloat16),
            pltpu.VMEM((2 * height, width), jnp.float32),
            pltpu.VMEM((2, INTERSECTION, width), jnp.float32),
            pltpu.VMEM((2, INTERSECTION, width), jnp.float32),
            dma((m, MATES)),
            dma((m, MATES)),
            dma((MATES,)),
            dma((MATES,)),
            dma((m,)),
            dma((m,)),
            dma((2,)),
        ],
        compiler_params=pltpu.CompilerParams(
            collective_id=0, has_side_effects=True, vmem_limit_bytes=VMEM_BYTES
        ),
        name="exchange",
    )(length, message, lines, tile)


def on_device(
    secondary_pieces,
    piece_target,
    piece_block,
    piece_row,
    piece_column,
    ramp_rate,
    centroid,
    sinc_blocks,
    reference_tile,
    intersection_rows,
):
    tile_count = lax.axis_size("az")
    capacity = max(2, 2 * secondary_pieces.shape[0] // tile_count)
    tables, taps = gather_tables(ramp_rate, centroid, sinc_blocks)
    coregistered, message, lines = resample(
        secondary_pieces,
        piece_target[:, 0],
        piece_block,
        piece_row,
        piece_column,
        tables,
        taps,
        capacity,
    )
    interferogram, diversity = exchange(message, lines, reference_tile, intersection_rows)
    return coregistered, interferogram, diversity


def solution(mesh):
    split = ("dates", "az")
    return jax.shard_map(
        on_device,
        mesh=mesh,
        in_specs=(
            P(split, None, None, None),
            P(split, None),
            P(split),
            P(split),
            P(split),
            P(split, None),
            P(split, None),
            P(),
            P(None, split, None),
            P(split),
        ),
        out_specs=(
            P(split, None, None, None),
            P(None, split, None),
            P(split, None, None),
        ),
        check_vma=False,
    )
```

```python
import functools

import jax
import jax.numpy as jnp
from jax import lax
from jax.experimental import pallas as pl
from jax.experimental.pallas import tpu as pltpu
from jax.sharding import PartitionSpec as P

TILE_ROWS = 256
INTERSECTION = 32
WEIGHT_BLOCKS = 64
GROUP = 16
MATES = 8
VMEM_BYTES = 63 * 1024 * 1024
MESH = pl.DeviceIdType.MESH

SIN_FIT = (6.2831807136535645, -41.33925247192383, 81.40833282470703, -71.61119079589844)
COS_FIT = (0.9999932646751404, -19.73573875427246, 64.65997314453125, -78.21002960205078)


def unit_phasor(turns):
    part = turns - jnp.round(turns)
    w = 0.25 - jnp.abs(part)
    w2 = w * w
    even = jnp.full_like(w2, COS_FIT[-1])
    for coeff in COS_FIT[-2::-1]:
        even = even * w2 + coeff
    odd = jnp.full_like(w2, SIN_FIT[-1])
    for coeff in SIN_FIT[-2::-1]:
        odd = odd * w2 + coeff
    return odd * w, jnp.where(part < 0, -even, even)


def resample_kernel(
    target_ref,
    block_ref,
    row_ref,
    col_ref,
    pieces_ref,
    table_ref,
    taps_hbm,
    out_ref,
    message_ref,
    lines_ref,
    deramped,
    band,
    mixed,
    used,
    target,
    block,
    row,
    col,
    pieces,
    taps_ref,
    fetch_sem,
    pieces_sem,
):
    step = pl.program_id(0)
    width = pieces_ref.shape[3]
    half = width // 2
    fetches = [
        pltpu.make_async_copy(source, scalars, fetch_sem.at[i])
        for i, (source, scalars) in enumerate(
            [
                (target_ref, target),
                (block_ref, block),
                (row_ref, row),
                (col_ref, col),
                (taps_hbm, taps_ref),
            ]
        )
    ]

    def pieces_copy(group):
        part = pl.ds(group * GROUP, GROUP)
        return pltpu.make_async_copy(
            pieces_ref.at[part], pieces.at[part], pieces_sem.at[group]
        )

    @pl.when(step == 0)
    def _():
        for fetch in fetches:
            fetch.start()

        @pl.loop(0, pieces_ref.shape[0] // GROUP)
        def _(group):
            pieces_copy(group).start()

        message_ref[...] = jnp.zeros_like(message_ref)
        band[...] = jnp.zeros_like(band)
        lines_ref[...] = jnp.full_like(lines_ref, -1)

        @pl.loop(0, used.shape[0])
        def _(tile):
            used[tile] = 0

        for fetch in fetches:
            fetch.wait()

    pieces_copy(step).wait()

    in_iota = lax.broadcasted_iota(jnp.int32, (16, width), 0).astype(jnp.float32)
    out_iota = lax.broadcasted_iota(jnp.int32, (8, width), 0).astype(jnp.float32)
    band_lane = lax.broadcasted_iota(jnp.int32, (64, 128), 1) // 16
    lane = lax.broadcasted_iota(jnp.int32, (8, half), 1)
    slot_lane = lax.broadcasted_iota(jnp.int32, (1, lines_ref.shape[2]), 1)
    slot_line = slot_lane % 8

    def table_rows(tile):
        return 0.5 * table_ref[tile, 0], table_ref[tile, 1]

    def before(i):
        p = step * GROUP + i
        rate, centre = table_rows(target[p])
        u = (in_iota + (row[p].astype(jnp.float32) - (3.0 + TILE_ROWS / 2))) * (1.0 / TILE_ROWS)
        cosine, sine = unit_phasor((rate * u + centre) * u)
        real = pieces[p, 0].astype(jnp.float32)
        imag = pieces[p, 1].astype(jnp.float32)
        lines = slice(i * 16, i * 16 + 16)
        deramped[lines, 0:width] = (real * cosine + imag * sine).astype(jnp.bfloat16)
        deramped[lines, width : 2 * width] = (imag * cosine - real * sine).astype(jnp.bfloat16)
        taps = taps_ref[block[p]]
        first = i // 8 * 128
        band[i * 64 : i * 64 + 64, first : first + 128] = jnp.where(
            band_lane == i % 8, taps, jnp.zeros_like(taps)
        )

    for i in range(GROUP):
        before(i)

    mixed[...] = jnp.dot(band[...], deramped[...], preferred_element_type=jnp.float32)

    def after(i):
        p = step * GROUP + i
        tile = target[p]
        shift0 = col[p] - 3
        sums = [jnp.zeros((8, half), jnp.float32) for _ in range(4)]
        for b in range(8):
            shift = shift0 + b
            turn = lax.rem(half - shift, half)
            place = lane + shift
            inside = (place >= 0) & (place < half)
            above = (shift > 0).astype(jnp.float32)
            below = (shift < 0).astype(jnp.float32)
            lines = slice(i * 64 + b * 8, i * 64 + b * 8 + 8)
            for z in range(2):
                left = pltpu.roll(mixed[lines, z * width : z * width + half], turn, 1)
                right = pltpu.roll(mixed[lines, z * width + half : (z + 1) * width], turn, 1)
                sums[2 * z] = sums[2 * z] + jnp.where(inside, left, right * above)
                sums[2 * z + 1] = sums[2 * z + 1] + jnp.where(inside, right, left * below)
        real = jnp.concatenate(sums[0:2], axis=1)
        imag = jnp.concatenate(sums[2:4], axis=1)
        rate, centre = table_rows(tile)
        start = (
            row[p].astype(jnp.float32)
            + block[p].astype(jnp.float32) * (1.0 / WEIGHT_BLOCKS)
            - TILE_ROWS / 2
        )
        u = (out_iota + start) * (1.0 / TILE_ROWS)
        cosine, sine = unit_phasor((rate * u + centre) * u)
        out_real = real * cosine - imag * sine
        out_imag = imag * cosine + real * sine
        out_ref[i, 0] = out_real.astype(jnp.bfloat16)
        out_ref[i, 1] = out_imag.astype(jnp.bfloat16)
        slot = used[tile]
        used[tile] = slot + 1
        message_ref[tile, pl.ds(pl.multiple_of(slot * 16, 16), 16), :] = jnp.concatenate(
            [out_real, out_imag], axis=0
        ).astype(jnp.bfloat16)
        mate, plane = lax.rem(tile, MATES), pl.ds(tile // MATES, 1)
        lines_ref[mate, plane, :] = jnp.where(
            slot_lane // 16 == slot, slot_line + row[p], lines_ref[mate, plane, :]
        )

    for i in range(GROUP):
        after(i)


def resample(pieces, target, block, row, col, tables, taps, capacity):
    count, _, _, width = pieces.shape
    tiles = tables.shape[0]
    rows = capacity * 16
    line_shape = (MATES, max(8, tiles // MATES), max(128, rows))
    whole = lambda *shape: pl.BlockSpec(shape, lambda g: (0,) * len(shape))
    remote = pl.BlockSpec(memory_space=pltpu.HBM)
    return pl.pallas_call(
        resample_kernel,
        grid_spec=pltpu.PrefetchScalarGridSpec(
            num_scalar_prefetch=0,
            grid=(count // GROUP,),
            in_specs=[
                *[remote] * 5,
                whole(*tables.shape),
                remote,
            ],
            out_specs=[
                pl.BlockSpec((GROUP, 2, 8, width), lambda g: (g, 0, 0, 0)),
                whole(tiles, rows, width),
                whole(*line_shape),
            ],
            scratch_shapes=[
                pltpu.VMEM((GROUP * 16, 2 * width), jnp.bfloat16),
                pltpu.VMEM((GROUP * 64, GROUP * 16), jnp.bfloat16),
                pltpu.VMEM((GROUP * 64, 2 * width), jnp.float32),
                pltpu.SMEM((tiles,), jnp.int32),
                *[pltpu.SMEM((count,), jnp.int32)] * 4,
                pltpu.VMEM(pieces.shape, jnp.bfloat16),
                pltpu.VMEM(taps.shape, jnp.bfloat16),
                pltpu.SemaphoreType.DMA((5,)),
                pltpu.SemaphoreType.DMA((count // GROUP,)),
            ],
        ),
        out_shape=[
            jax.ShapeDtypeStruct((count, 2, 8, width), jnp.bfloat16),
            jax.ShapeDtypeStruct((tiles, rows, width), jnp.bfloat16),
            jax.ShapeDtypeStruct(line_shape, jnp.int32),
        ],
        compiler_params=pltpu.CompilerParams(
            dimension_semantics=("arbitrary",), vmem_limit_bytes=VMEM_BYTES
        ),
        name="resample",
    )(target, block, row, col, pieces, tables, taps)


def gather_kernel(
    n,
    rate_ref,
    centre_ref,
    sinc_ref,
    out_ref,
    taps_ref,
    own,
    got,
    sinc,
    wide,
    fetch_sem,
    send_sem,
    recv_sem,
):
    me = lax.axis_index("az")
    fetches = [
        pltpu.make_async_copy(rate_ref, own.at[0], fetch_sem.at[0]),
        pltpu.make_async_copy(centre_ref, own.at[1], fetch_sem.at[1]),
        pltpu.make_async_copy(sinc_ref, sinc, fetch_sem.at[2]),
    ]
    for fetch in fetches:
        fetch.start()
    barrier = pltpu.get_barrier_semaphore()

    def to_all(k):
        to = lax.rem(me + k, n)
        return pltpu.make_async_remote_copy(
            src_ref=own,
            dst_ref=got.at[me],
            send_sem=send_sem.at[k],
            recv_sem=recv_sem.at[k],
            device_id={"az": to},
            device_id_type=MESH,
        )

    def from_all(k):
        return pltpu.make_async_remote_copy(
            src_ref=own,
            dst_ref=got.at[lax.rem(me - k + n, n)],
            send_sem=send_sem.at[k],
            recv_sem=recv_sem.at[k],
            device_id={"az": lax.rem(me + k, n)},
            device_id_type=MESH,
        )

    @pl.loop(1, n)
    def _(k):
        pl.semaphore_signal(
            barrier, inc=1, device_id={"az": lax.rem(me + k, n)}, device_id_type=MESH
        )

    fetches[0].wait()
    fetches[1].wait()
    got[me] = own[...]
    pl.semaphore_wait(barrier, n - 1)

    @pl.loop(1, n)
    def _(k):
        to_all(k).start()

    fetches[2].wait()
    blocks = sinc_ref.shape[2]
    place = (
        lax.broadcasted_iota(jnp.int32, (8, 128), 1) % 16
        == lax.broadcasted_iota(jnp.int32, (8, 128), 0)
    ).astype(jnp.float32)
    for b in range(8):
        wide[b] = lax.dot_general(
            sinc[:, b, :],
            place,
            (((0,), (0,)), ((), ())),
            preferred_element_type=jnp.float32,
        )

    @pl.loop(0, blocks)
    def _(block):
        for b in range(0, 8, 2):
            pair = jnp.concatenate(
                [
                    pltpu.roll(
                        jnp.broadcast_to(wide[b + e, pl.ds(block, 1), :], (8, 128)),
                        0,
                        1,
                        stride=1,
                        stride_axis=0,
                    )
                    for e in range(2)
                ],
                axis=0,
            ).astype(jnp.bfloat16)
            taps_ref[block, b * 8 : b * 8 + 16, :] = pair

    @pl.loop(1, n)
    def _(k):
        from_all(k).wait_recv()

    out_ref[...] = got[...]

    @pl.loop(1, n)
    def _(k):
        to_all(k).wait_send()


def gather_tables(rate, centre, sinc_blocks):
    n = lax.axis_size("az")
    width = rate.shape[1]
    blocks = sinc_blocks.shape[0]
    return pl.pallas_call(
        functools.partial(gather_kernel, n),
        in_specs=[pl.BlockSpec(memory_space=pltpu.HBM)] * 3,
        out_specs=[pl.BlockSpec(memory_space=pltpu.VMEM)] * 2,
        out_shape=[
            jax.ShapeDtypeStruct((n, 2, 1, width), jnp.float32),
            jax.ShapeDtypeStruct((blocks, 64, 128), jnp.bfloat16),
        ],
        scratch_shapes=[
            pltpu.VMEM((2, 1, width), jnp.float32),
            pltpu.VMEM((n, 2, 1, width), jnp.float32),
            pltpu.VMEM((8, 8, blocks), jnp.float32),
            pltpu.VMEM((8, blocks, 128), jnp.float32),
            pltpu.SemaphoreType.DMA((3,)),
            pltpu.SemaphoreType.DMA((n,)),
            pltpu.SemaphoreType.DMA((n,)),
        ],
        compiler_params=pltpu.CompilerParams(
            collective_id=1, has_side_effects=True, vmem_limit_bytes=VMEM_BYTES
        ),
        name="gather_tables",
    )(rate, centre, jnp.transpose(sinc_blocks, (1, 2, 0)))


def exchange_kernel(
    n,
    length_ref,
    message_ref,
    lines_hbm,
    tile_hbm,
    out_ref,
    sum_ref,
    lines_ref,
    tile_ref,
    own_sem,
    got,
    got_lines,
    part,
    got_part,
    total,
    tail,
    previous,
    send_sem,
    recv_sem,
    lines_send_sem,
    lines_recv_sem,
    part_send_sem,
    part_recv_sem,
    tail_sem,
):
    me = lax.axis_index("az")
    height = tile_hbm.shape[1]
    rows, width = message_ref.shape[1:]
    m = n // MATES
    lines_fetch = pltpu.make_async_copy(lines_hbm, lines_ref, own_sem.at[0])
    tile_fetch = pltpu.make_async_copy(tile_hbm, tile_ref, own_sem.at[1])
    lines_fetch.start()
    tile_fetch.start()
    high, low = me // MATES, lax.rem(me, MATES)

    def mate(e):
        return high * MATES + lax.rem(low + e, MATES)

    def peer(k):
        return lax.rem(high + k, m) * MATES + low

    def lines_copy(e):
        return pltpu.make_async_remote_copy(
            src_ref=lines_ref.at[lax.rem(low + e, MATES)],
            dst_ref=got_lines.at[e],
            send_sem=lines_send_sem.at[e],
            recv_sem=lines_recv_sem.at[e],
            device_id={"az": mate(e)},
            device_id_type=MESH,
        )

    def data_copy(k, e):
        tile = lax.rem(high + k, m) * MATES + lax.rem(low + e, MATES)
        return pltpu.make_async_remote_copy(
            src_ref=message_ref.at[tile],
            dst_ref=got.at[k, e],
            send_sem=send_sem.at[k, e],
            recv_sem=recv_sem.at[k, e],
            device_id={"az": mate(e)},
            device_id_type=MESH,
        )

    def own_copy(k):
        return pltpu.make_async_copy(message_ref.at[peer(k)], got.at[k, 0], own_sem.at[2 + k])

    def part_copy(k):
        return pltpu.make_async_remote_copy(
            src_ref=part.at[k],
            dst_ref=got_part.at[k],
            send_sem=part_send_sem.at[k],
            recv_sem=part_recv_sem.at[k],
            device_id={"az": peer(k)},
            device_id_type=MESH,
        )

    tail_copy = pltpu.make_async_remote_copy(
        src_ref=tail,
        dst_ref=previous,
        send_sem=tail_sem.at[0],
        recv_sem=tail_sem.at[1],
        device_id={"az": lax.rem(me + 1, n)},
        device_id_type=MESH,
    )

    @pl.loop(0, m)
    def _(k):
        own_copy(k).start()

    barrier = pltpu.get_barrier_semaphore()
    for e in range(1, MATES):
        pl.semaphore_signal(barrier, inc=1, device_id={"az": mate(e)}, device_id_type=MESH)

    @pl.loop(1, m)
    def _(k):
        pl.semaphore_signal(barrier, inc=1, device_id={"az": peer(k)}, device_id_type=MESH)

    @pl.when(low == 0)
    def _():
        pl.semaphore_signal(
            barrier, inc=1, device_id={"az": lax.rem(me + n - 1, n)}, device_id_type=MESH
        )

    @pl.when(me == 0)
    def _():
        previous[...] = jnp.zeros_like(previous)

    pl.semaphore_wait(barrier, MATES - 1 + m - 1 + low // (MATES - 1))

    lines_fetch.wait()
    for e in range(1, MATES):
        lines_copy(e).start()

    def order(j):
        return 1 + lax.rem(j + m // 2 - 1, m - 1) if m > 1 else 0

    for e in range(1, MATES):
        data_copy(order(0), e).start()

    def as_bf16(value):
        return value.astype(jnp.float32).astype(jnp.bfloat16)

    wanted = as_bf16(lax.broadcasted_iota(jnp.int32, (height, rows), 0))
    channel = lax.broadcasted_iota(jnp.int32, (rows, width), 0) // 8 % 2
    is_imag = as_bf16(channel)
    is_real = as_bf16(1 - channel)

    def placed(lines, data):
        one = jnp.ones((), jnp.bfloat16)
        pick = jnp.where(wanted == as_bf16(lines), one, jnp.zeros_like(one))
        both = jnp.concatenate([data * is_real, data * is_imag], axis=1)
        return jnp.dot(pick, both, preferred_element_type=jnp.float32)

    def summed(k):
        plane = lax.rem(high + k, m)
        own_copy(k).wait()
        result = placed(lines_ref[low, pl.ds(plane, 1), 0:rows], got[k, 0])
        for e in range(1, MATES):
            data_copy(k, e).wait_recv()
            result = result + placed(got_lines[e, pl.ds(plane, 1), 0:rows], got[k, e])
        return result

    for e in range(1, MATES):
        lines_copy(e).wait_recv()

    @pl.loop(0, m - 1)
    def _(j):
        k = order(j)
        following = jnp.where(j + 1 == m - 1, 0, order(j + 1))
        for e in range(1, MATES):
            data_copy(k, e).wait_send()
            data_copy(following, e).start()
        part[k] = summed(k).astype(jnp.bfloat16)
        part_copy(k).start()

    total[...] = summed(0)

    @pl.loop(0, m - 1)
    def _(j):
        k = order(j)
        part_copy(k).wait_recv()
        total[...] += got_part[k].astype(jnp.float32)

    tile_fetch.wait()
    ref_real, ref_imag = tile_ref[0], tile_ref[1]
    got_real, got_imag = total[:, 0:width], total[:, width : 2 * width]
    out_ref[0] = ref_real * got_real + ref_imag * got_imag
    out_ref[1] = ref_imag * got_real - ref_real * got_imag
    tail[...] = out_ref[:, height - INTERSECTION : height, :]

    @pl.when(me < n - 1)
    def _():
        tail_copy.start()

    length = length_ref[0]
    apart = lax.broadcasted_iota(
        jnp.int32, (INTERSECTION, INTERSECTION), 1
    ) - lax.broadcasted_iota(jnp.int32, (INTERSECTION, INTERSECTION), 0)
    shifter = (apart == INTERSECTION - length).astype(jnp.float32)

    @pl.when(me > 0)
    def _():
        tail_copy.wait_recv()

    before = [
        jnp.dot(
            shifter,
            previous[z],
            precision=lax.Precision.HIGHEST,
            preferred_element_type=jnp.float32,
        )
        for z in range(2)
    ]
    head = [out_ref[z, 0:INTERSECTION, :] for z in range(2)]
    scale = 1.0 / length.astype(jnp.float32)
    sum_ref[0, 0:1, :] = scale * jnp.sum(
        head[0] * before[0] + head[1] * before[1], axis=0, keepdims=True
    )
    sum_ref[0, 1:2, :] = scale * jnp.sum(
        head[1] * before[0] - head[0] * before[1], axis=0, keepdims=True
    )

    for e in range(1, MATES):
        lines_copy(e).wait_send()

    for e in range(1, MATES):
        data_copy(0, e).wait_send()

    @pl.loop(1, m)
    def _(k):
        part_copy(k).wait_send()

    @pl.when(me < n - 1)
    def _():
        tail_copy.wait_send()


def exchange(message, lines, tile, length):
    n, rows, width = message.shape
    height = tile.shape[1]
    m = n // MATES
    dma = pltpu.SemaphoreType.DMA
    return pl.pallas_call(
        functools.partial(exchange_kernel, n),
        in_specs=[pl.BlockSpec(memory_space=pltpu.SMEM)]
        + [pl.BlockSpec(memory_space=pltpu.HBM)] * 3,
        out_specs=[pl.BlockSpec(memory_space=pltpu.VMEM)] * 2,
        out_shape=[
            jax.ShapeDtypeStruct(tile.shape, jnp.float32),
            jax.ShapeDtypeStruct((1, 2, width), jnp.float32),
        ],
        scratch_shapes=[
            pltpu.VMEM(lines.shape, jnp.int32),
            pltpu.VMEM(tile.shape, jnp.float32),
            dma((2 + m,)),
            pltpu.VMEM((m, MATES, rows, width), jnp.bfloat16),
            pltpu.VMEM(lines.shape, jnp.int32),
            pltpu.VMEM((m, height, 2 * width), jnp.bfloat16),
            pltpu.VMEM((m, height, 2 * width), jnp.bfloat16),
            pltpu.VMEM((height, 2 * width), jnp.float32),
            pltpu.VMEM((2, INTERSECTION, width), jnp.float32),
            pltpu.VMEM((2, INTERSECTION, width), jnp.float32),
            dma((m, MATES)),
            dma((m, MATES)),
            dma((MATES,)),
            dma((MATES,)),
            dma((m,)),
            dma((m,)),
            dma((2,)),
        ],
        compiler_params=pltpu.CompilerParams(
            collective_id=0, has_side_effects=True, vmem_limit_bytes=VMEM_BYTES
        ),
        name="exchange",
    )(length, message, lines, tile)


def on_device(
    secondary_pieces,
    piece_target,
    piece_block,
    piece_row,
    piece_column,
    ramp_rate,
    centroid,
    sinc_blocks,
    reference_tile,
    intersection_rows,
):
    tile_count = lax.axis_size("az")
    capacity = max(2, 2 * secondary_pieces.shape[0] // tile_count)
    tables, taps = gather_tables(ramp_rate, centroid, sinc_blocks)
    coregistered, message, lines = resample(
        secondary_pieces,
        piece_target[:, 0],
        piece_block,
        piece_row,
        piece_column,
        tables,
        taps,
        capacity,
    )
    interferogram, diversity = exchange(message, lines, reference_tile, intersection_rows)
    return coregistered, interferogram, diversity


def solution(mesh):
    split = ("dates", "az")
    return jax.shard_map(
        on_device,
        mesh=mesh,
        in_specs=(
            P(split, None, None, None),
            P(split, None),
            P(split),
            P(split),
            P(split),
            P(split, None),
            P(split, None),
            P(),
            P(None, split, None),
            P(split),
        ),
        out_specs=(
            P(split, None, None, None),
            P(None, split, None),
            P(split, None, None),
        ),
        check_vma=False,
    )
```

```python
import functools

import jax
import jax.numpy as jnp
from jax import lax
from jax.experimental import pallas as pl
from jax.experimental.pallas import tpu as pltpu
from jax.sharding import PartitionSpec as P

TILE_ROWS = 256
INTERSECTION = 32
WEIGHT_BLOCKS = 64
GROUP = 16
MATES = 8
VMEM_BYTES = 63 * 1024 * 1024
EXCHANGE_BYTES = 53 * 1024 * 1024
MESH = pl.DeviceIdType.MESH

SIN_FIT = (6.2831807136535645, -41.33925247192383, 81.40833282470703, -71.61119079589844)
COS_FIT = (0.9999932646751404, -19.73573875427246, 64.65997314453125, -78.21002960205078)


def unit_phasor(turns):
    part = turns - jnp.round(turns)
    w = 0.25 - jnp.abs(part)
    w2 = w * w
    even = jnp.full_like(w2, COS_FIT[-1])
    for coeff in COS_FIT[-2::-1]:
        even = even * w2 + coeff
    odd = jnp.full_like(w2, SIN_FIT[-1])
    for coeff in SIN_FIT[-2::-1]:
        odd = odd * w2 + coeff
    return odd * w, jnp.where(part < 0, -even, even)


def resample_kernel(
    target_ref,
    block_ref,
    row_ref,
    col_ref,
    pieces_ref,
    table_ref,
    taps_hbm,
    out_ref,
    message_ref,
    lines_ref,
    deramped_a,
    band_a,
    mixed_a,
    deramped_b,
    band_b,
    mixed_b,
    used,
    target,
    block,
    row,
    col,
    pieces,
    taps_ref,
    fetch_sem,
    pieces_sem,
):
    step = pl.program_id(0)
    width = pieces_ref.shape[3]
    half = width // 2
    fetches = [
        pltpu.make_async_copy(source, scalars, fetch_sem.at[i])
        for i, (source, scalars) in enumerate(
            [
                (target_ref, target),
                (block_ref, block),
                (row_ref, row),
                (col_ref, col),
                (taps_hbm, taps_ref),
            ]
        )
    ]

    def pieces_copy(group):
        part = pl.ds(group * GROUP, GROUP)
        return pltpu.make_async_copy(
            pieces_ref.at[part], pieces.at[part], pieces_sem.at[group]
        )

    @pl.when(step == 0)
    def _():
        for fetch in fetches:
            fetch.start()

        @pl.loop(0, pieces_ref.shape[0] // GROUP)
        def _(group):
            pieces_copy(group).start()

        message_ref[...] = jnp.zeros_like(message_ref)
        band_a[...] = jnp.zeros_like(band_a)
        band_b[...] = jnp.zeros_like(band_b)
        lines_ref[...] = jnp.full_like(lines_ref, -1)

        @pl.loop(0, used.shape[0])
        def _(tile):
            used[tile] = 0

        for fetch in fetches:
            fetch.wait()

    pieces_copy(2 * step).wait()
    pieces_copy(2 * step + 1).wait()

    in_iota = lax.broadcasted_iota(jnp.int32, (16, width), 0).astype(jnp.float32)
    out_iota = lax.broadcasted_iota(jnp.int32, (8, width), 0).astype(jnp.float32)
    band_lane = lax.broadcasted_iota(jnp.int32, (64, 128), 1) // 16
    lane = lax.broadcasted_iota(jnp.int32, (8, half), 1)
    slot_lane = lax.broadcasted_iota(jnp.int32, (1, lines_ref.shape[2]), 1)
    slot_line = slot_lane % 8

    def table_rows(tile):
        return 0.5 * table_ref[tile, 0], table_ref[tile, 1]

    def before(part, i, deramped, band):
        p = (2 * step + part) * GROUP + i
        rate, centre = table_rows(target[p])
        u = (in_iota + (row[p].astype(jnp.float32) - (3.0 + TILE_ROWS / 2))) * (1.0 / TILE_ROWS)
        cosine, sine = unit_phasor((rate * u + centre) * u)
        real = pieces[p, 0].astype(jnp.float32)
        imag = pieces[p, 1].astype(jnp.float32)
        lines = slice(i * 16, i * 16 + 16)
        deramped[lines, 0:width] = (real * cosine + imag * sine).astype(jnp.bfloat16)
        deramped[lines, width : 2 * width] = (imag * cosine - real * sine).astype(jnp.bfloat16)
        taps = taps_ref[block[p]]
        first = i // 8 * 128
        band[i * 64 : i * 64 + 64, first : first + 128] = jnp.where(
            band_lane == i % 8, taps, jnp.zeros_like(taps)
        )


    def after(part, i, mixed):
        p = (2 * step + part) * GROUP + i
        tile = target[p]
        shift0 = col[p] - 3
        sums = [jnp.zeros((8, half), jnp.float32) for _ in range(4)]
        for b in range(8):
            shift = shift0 + b
            turn = lax.rem(half - shift, half)
            place = lane + shift
            inside = (place >= 0) & (place < half)
            above = (shift > 0).astype(jnp.float32)
            below = (shift < 0).astype(jnp.float32)
            lines = slice(i * 64 + b * 8, i * 64 + b * 8 + 8)
            for z in range(2):
                left = pltpu.roll(mixed[lines, z * width : z * width + half], turn, 1)
                right = pltpu.roll(mixed[lines, z * width + half : (z + 1) * width], turn, 1)
                sums[2 * z] = sums[2 * z] + jnp.where(inside, left, right * above)
                sums[2 * z + 1] = sums[2 * z + 1] + jnp.where(inside, right, left * below)
        real = jnp.concatenate(sums[0:2], axis=1)
        imag = jnp.concatenate(sums[2:4], axis=1)
        rate, centre = table_rows(tile)
        start = (
            row[p].astype(jnp.float32)
            + block[p].astype(jnp.float32) * (1.0 / WEIGHT_BLOCKS)
            - TILE_ROWS / 2
        )
        u = (out_iota + start) * (1.0 / TILE_ROWS)
        cosine, sine = unit_phasor((rate * u + centre) * u)
        out_real = real * cosine - imag * sine
        out_imag = imag * cosine + real * sine
        out_ref[part * GROUP + i, 0] = out_real.astype(jnp.bfloat16)
        out_ref[part * GROUP + i, 1] = out_imag.astype(jnp.bfloat16)
        slot = used[tile]
        used[tile] = slot + 1
        message_ref[tile, pl.ds(pl.multiple_of(slot * 16, 16), 16), :] = jnp.concatenate(
            [out_real, out_imag], axis=0
        ).astype(jnp.bfloat16)
        mate, plane = lax.rem(tile, MATES), pl.ds(tile // MATES, 1)
        lines_ref[mate, plane, :] = jnp.where(
            slot_lane // 16 == slot, slot_line + row[p], lines_ref[mate, plane, :]
        )

    def mix(deramped, band, mixed):
        mixed[...] = jnp.dot(band[...], deramped[...], preferred_element_type=jnp.float32)

    for i in range(GROUP):
        before(0, i, deramped_a, band_a)
    mix(deramped_a, band_a, mixed_a)
    for i in range(GROUP):
        before(1, i, deramped_b, band_b)
    mix(deramped_b, band_b, mixed_b)
    for i in range(GROUP):
        after(0, i, mixed_a)
    for i in range(GROUP):
        after(1, i, mixed_b)


def resample(pieces, target, block, row, col, tables, taps, capacity):
    count, _, _, width = pieces.shape
    tiles = tables.shape[0]
    rows = capacity * 16
    line_shape = (MATES, max(8, tiles // MATES), max(128, rows))
    whole = lambda *shape: pl.BlockSpec(shape, lambda g: (0,) * len(shape))
    remote = pl.BlockSpec(memory_space=pltpu.HBM)
    return pl.pallas_call(
        resample_kernel,
        grid_spec=pltpu.PrefetchScalarGridSpec(
            num_scalar_prefetch=0,
            grid=(count // (2 * GROUP),),
            in_specs=[
                *[remote] * 5,
                whole(*tables.shape),
                remote,
            ],
            out_specs=[
                pl.BlockSpec((2 * GROUP, 2, 8, width), lambda g: (g, 0, 0, 0)),
                whole(tiles, rows, width),
                whole(*line_shape),
            ],
            scratch_shapes=[
                *[
                    pltpu.VMEM((GROUP * 16, 2 * width), jnp.bfloat16),
                    pltpu.VMEM((GROUP * 64, GROUP * 16), jnp.bfloat16),
                    pltpu.VMEM((GROUP * 64, 2 * width), jnp.float32),
                ]
                * 2,
                pltpu.SMEM((tiles,), jnp.int32),
                *[pltpu.SMEM((count,), jnp.int32)] * 4,
                pltpu.VMEM(pieces.shape, jnp.bfloat16),
                pltpu.VMEM(taps.shape, jnp.bfloat16),
                pltpu.SemaphoreType.DMA((5,)),
                pltpu.SemaphoreType.DMA((count // GROUP,)),
            ],
        ),
        out_shape=[
            jax.ShapeDtypeStruct((count, 2, 8, width), jnp.bfloat16),
            jax.ShapeDtypeStruct((tiles, rows, width), jnp.bfloat16),
            jax.ShapeDtypeStruct(line_shape, jnp.int32),
        ],
        compiler_params=pltpu.CompilerParams(
            dimension_semantics=("arbitrary",), vmem_limit_bytes=VMEM_BYTES
        ),
        name="resample",
    )(target, block, row, col, pieces, tables, taps)


def gather_kernel(
    n,
    rate_ref,
    centre_ref,
    sinc_ref,
    out_ref,
    taps_ref,
    own,
    got,
    sinc,
    wide,
    fetch_sem,
    send_sem,
    recv_sem,
):
    me = lax.axis_index("az")
    fetches = [
        pltpu.make_async_copy(rate_ref, own.at[0], fetch_sem.at[0]),
        pltpu.make_async_copy(centre_ref, own.at[1], fetch_sem.at[1]),
        pltpu.make_async_copy(sinc_ref, sinc, fetch_sem.at[2]),
    ]
    for fetch in fetches:
        fetch.start()
    barrier = pltpu.get_barrier_semaphore()

    def to_all(k):
        to = lax.rem(me + k, n)
        return pltpu.make_async_remote_copy(
            src_ref=own,
            dst_ref=got.at[me],
            send_sem=send_sem.at[k],
            recv_sem=recv_sem.at[k],
            device_id={"az": to},
            device_id_type=MESH,
        )

    def from_all(k):
        return pltpu.make_async_remote_copy(
            src_ref=own,
            dst_ref=got.at[lax.rem(me - k + n, n)],
            send_sem=send_sem.at[k],
            recv_sem=recv_sem.at[k],
            device_id={"az": lax.rem(me + k, n)},
            device_id_type=MESH,
        )

    @pl.loop(1, n)
    def _(k):
        pl.semaphore_signal(
            barrier, inc=1, device_id={"az": lax.rem(me + k, n)}, device_id_type=MESH
        )

    fetches[0].wait()
    fetches[1].wait()
    got[me] = own[...]
    pl.semaphore_wait(barrier, n - 1)

    @pl.loop(1, n)
    def _(k):
        to_all(k).start()

    fetches[2].wait()
    blocks = sinc_ref.shape[2]
    place = (
        lax.broadcasted_iota(jnp.int32, (8, 128), 1) % 16
        == lax.broadcasted_iota(jnp.int32, (8, 128), 0)
    ).astype(jnp.float32)
    for b in range(8):
        wide[b] = lax.dot_general(
            sinc[:, b, :],
            place,
            (((0,), (0,)), ((), ())),
            preferred_element_type=jnp.float32,
        )

    @pl.loop(0, blocks)
    def _(block):
        for b in range(0, 8, 2):
            pair = jnp.concatenate(
                [
                    pltpu.roll(
                        jnp.broadcast_to(wide[b + e, pl.ds(block, 1), :], (8, 128)),
                        0,
                        1,
                        stride=1,
                        stride_axis=0,
                    )
                    for e in range(2)
                ],
                axis=0,
            ).astype(jnp.bfloat16)
            taps_ref[block, b * 8 : b * 8 + 16, :] = pair

    @pl.loop(1, n)
    def _(k):
        from_all(k).wait_recv()

    out_ref[...] = got[...]

    @pl.loop(1, n)
    def _(k):
        to_all(k).wait_send()


def gather_tables(rate, centre, sinc_blocks):
    n = lax.axis_size("az")
    width = rate.shape[1]
    blocks = sinc_blocks.shape[0]
    return pl.pallas_call(
        functools.partial(gather_kernel, n),
        in_specs=[pl.BlockSpec(memory_space=pltpu.HBM)] * 3,
        out_specs=[pl.BlockSpec(memory_space=pltpu.VMEM)] * 2,
        out_shape=[
            jax.ShapeDtypeStruct((n, 2, 1, width), jnp.float32),
            jax.ShapeDtypeStruct((blocks, 64, 128), jnp.bfloat16),
        ],
        scratch_shapes=[
            pltpu.VMEM((2, 1, width), jnp.float32),
            pltpu.VMEM((n, 2, 1, width), jnp.float32),
            pltpu.VMEM((8, 8, blocks), jnp.float32),
            pltpu.VMEM((8, blocks, 128), jnp.float32),
            pltpu.SemaphoreType.DMA((3,)),
            pltpu.SemaphoreType.DMA((n,)),
            pltpu.SemaphoreType.DMA((n,)),
        ],
        compiler_params=pltpu.CompilerParams(
            collective_id=1, has_side_effects=True, vmem_limit_bytes=VMEM_BYTES
        ),
        name="gather_tables",
    )(rate, centre, jnp.transpose(sinc_blocks, (1, 2, 0)))


def exchange_kernel(
    n,
    length_ref,
    message_ref,
    lines_hbm,
    tile_hbm,
    out_ref,
    sum_ref,
    lines_ref,
    tile_ref,
    own_sem,
    got,
    got_lines,
    part,
    got_part,
    total,
    tail,
    previous,
    send_sem,
    recv_sem,
    lines_send_sem,
    lines_recv_sem,
    part_send_sem,
    part_recv_sem,
    tail_sem,
):
    me = lax.axis_index("az")
    height = tile_hbm.shape[1]
    rows, width = message_ref.shape[1:]
    m = n // MATES
    lines_fetch = pltpu.make_async_copy(lines_hbm, lines_ref, own_sem.at[0])
    tile_fetch = pltpu.make_async_copy(tile_hbm, tile_ref, own_sem.at[1])
    lines_fetch.start()
    tile_fetch.start()
    high, low = me // MATES, lax.rem(me, MATES)

    def mate(e):
        return high * MATES + lax.rem(low + e, MATES)

    def peer(k):
        return lax.rem(high + k, m) * MATES + low

    def lines_copy(e):
        return pltpu.make_async_remote_copy(
            src_ref=lines_ref.at[lax.rem(low + e, MATES)],
            dst_ref=got_lines.at[e],
            send_sem=lines_send_sem.at[e],
            recv_sem=lines_recv_sem.at[e],
            device_id={"az": mate(e)},
            device_id_type=MESH,
        )

    def data_copy(k, e):
        tile = lax.rem(high + k, m) * MATES + lax.rem(low + e, MATES)
        return pltpu.make_async_remote_copy(
            src_ref=message_ref.at[tile],
            dst_ref=got.at[k, e],
            send_sem=send_sem.at[k, e],
            recv_sem=recv_sem.at[k, e],
            device_id={"az": mate(e)},
            device_id_type=MESH,
        )

    def own_copy(k):
        return pltpu.make_async_copy(message_ref.at[peer(k)], got.at[k, 0], own_sem.at[2 + k])

    def part_copy(k):
        return pltpu.make_async_remote_copy(
            src_ref=part.at[k],
            dst_ref=got_part.at[k],
            send_sem=part_send_sem.at[k],
            recv_sem=part_recv_sem.at[k],
            device_id={"az": peer(k)},
            device_id_type=MESH,
        )

    tail_copy = pltpu.make_async_remote_copy(
        src_ref=tail,
        dst_ref=previous,
        send_sem=tail_sem.at[0],
        recv_sem=tail_sem.at[1],
        device_id={"az": lax.rem(me + 1, n)},
        device_id_type=MESH,
    )

    @pl.loop(0, m)
    def _(k):
        own_copy(k).start()

    barrier = pltpu.get_barrier_semaphore()
    for e in range(1, MATES):
        pl.semaphore_signal(barrier, inc=1, device_id={"az": mate(e)}, device_id_type=MESH)

    @pl.loop(1, m)
    def _(k):
        pl.semaphore_signal(barrier, inc=1, device_id={"az": peer(k)}, device_id_type=MESH)

    @pl.when(low == 0)
    def _():
        pl.semaphore_signal(
            barrier, inc=1, device_id={"az": lax.rem(me + n - 1, n)}, device_id_type=MESH
        )

    @pl.when(me == 0)
    def _():
        previous[...] = jnp.zeros_like(previous)

    pl.semaphore_wait(barrier, MATES - 1 + m - 1 + low // (MATES - 1))

    lines_fetch.wait()
    for e in range(1, MATES):
        lines_copy(e).start()

    def order(j):
        return 1 + lax.rem(j + m // 2 - 1, m - 1) if m > 1 else 0

    for e in range(1, MATES):
        data_copy(order(0), e).start()

    def as_bf16(value):
        return value.astype(jnp.float32).astype(jnp.bfloat16)

    wanted = as_bf16(lax.broadcasted_iota(jnp.int32, (height, rows), 0))
    channel = lax.broadcasted_iota(jnp.int32, (rows, width), 0) // 8 % 2
    is_imag = as_bf16(channel)
    is_real = as_bf16(1 - channel)

    def placed(lines, data):
        one = jnp.ones((), jnp.bfloat16)
        pick = jnp.where(wanted == as_bf16(lines), one, jnp.zeros_like(one))
        both = jnp.concatenate([data * is_real, data * is_imag], axis=1)
        return jnp.dot(pick, both, preferred_element_type=jnp.float32)

    def summed(k):
        plane = lax.rem(high + k, m)
        own_copy(k).wait()
        result = placed(lines_ref[low, pl.ds(plane, 1), 0:rows], got[k, 0])
        for e in range(1, MATES):
            data_copy(k, e).wait_recv()
            result = result + placed(got_lines[e, pl.ds(plane, 1), 0:rows], got[k, e])
        return result

    for e in range(1, MATES):
        lines_copy(e).wait_recv()

    @pl.loop(0, m - 1)
    def _(j):
        k = order(j)
        following = jnp.where(j + 1 == m - 1, 0, order(j + 1))
        for e in range(1, MATES):
            data_copy(k, e).wait_send()
            data_copy(following, e).start()
        part[k] = summed(k).astype(jnp.bfloat16)
        part_copy(k).start()

    total[...] = summed(0)

    @pl.loop(0, m - 1)
    def _(j):
        k = order(j)
        part_copy(k).wait_recv()
        total[...] += got_part[k].astype(jnp.float32)

    tile_fetch.wait()
    ref_real, ref_imag = tile_ref[0], tile_ref[1]
    got_real, got_imag = total[:, 0:width], total[:, width : 2 * width]
    last = slice(height - INTERSECTION, height)
    tail[0] = ref_real[last] * got_real[last] + ref_imag[last] * got_imag[last]
    tail[1] = ref_imag[last] * got_real[last] - ref_real[last] * got_imag[last]

    @pl.when(me < n - 1)
    def _():
        tail_copy.start()

    out_ref[0] = ref_real * got_real + ref_imag * got_imag
    out_ref[1] = ref_imag * got_real - ref_real * got_imag

    length = length_ref[0]
    apart = lax.broadcasted_iota(
        jnp.int32, (INTERSECTION, INTERSECTION), 1
    ) - lax.broadcasted_iota(jnp.int32, (INTERSECTION, INTERSECTION), 0)
    shifter = (apart == INTERSECTION - length).astype(jnp.float32)

    @pl.when(me > 0)
    def _():
        tail_copy.wait_recv()

    before = [
        jnp.dot(
            shifter,
            previous[z],
            precision=lax.Precision.HIGHEST,
            preferred_element_type=jnp.float32,
        )
        for z in range(2)
    ]
    head = [out_ref[z, 0:INTERSECTION, :] for z in range(2)]
    scale = 1.0 / length.astype(jnp.float32)
    sum_ref[0, 0:1, :] = scale * jnp.sum(
        head[0] * before[0] + head[1] * before[1], axis=0, keepdims=True
    )
    sum_ref[0, 1:2, :] = scale * jnp.sum(
        head[1] * before[0] - head[0] * before[1], axis=0, keepdims=True
    )

    for e in range(1, MATES):
        lines_copy(e).wait_send()

    for e in range(1, MATES):
        data_copy(0, e).wait_send()

    @pl.loop(1, m)
    def _(k):
        part_copy(k).wait_send()

    @pl.when(me < n - 1)
    def _():
        tail_copy.wait_send()


def exchange(message, lines, tile, length):
    n, rows, width = message.shape
    height = tile.shape[1]
    m = n // MATES
    dma = pltpu.SemaphoreType.DMA
    return pl.pallas_call(
        functools.partial(exchange_kernel, n),
        in_specs=[pl.BlockSpec(memory_space=pltpu.SMEM)]
        + [pl.BlockSpec(memory_space=pltpu.HBM)] * 3,
        out_specs=[pl.BlockSpec(memory_space=pltpu.VMEM)] * 2,
        out_shape=[
            jax.ShapeDtypeStruct(tile.shape, jnp.float32),
            jax.ShapeDtypeStruct((1, 2, width), jnp.float32),
        ],
        scratch_shapes=[
            pltpu.VMEM(lines.shape, jnp.int32),
            pltpu.VMEM(tile.shape, jnp.float32),
            dma((2 + m,)),
            pltpu.VMEM((m, MATES, rows, width), jnp.bfloat16),
            pltpu.VMEM(lines.shape, jnp.int32),
            pltpu.VMEM((m, height, 2 * width), jnp.bfloat16),
            pltpu.VMEM((m, height, 2 * width), jnp.bfloat16),
            pltpu.VMEM((height, 2 * width), jnp.float32),
            pltpu.VMEM((2, INTERSECTION, width), jnp.float32),
            pltpu.VMEM((2, INTERSECTION, width), jnp.float32),
            dma((m, MATES)),
            dma((m, MATES)),
            dma((MATES,)),
            dma((MATES,)),
            dma((m,)),
            dma((m,)),
            dma((2,)),
        ],
        compiler_params=pltpu.CompilerParams(
            collective_id=0, has_side_effects=True, vmem_limit_bytes=EXCHANGE_BYTES
        ),
        name="exchange",
    )(length, message, lines, tile)


def on_device(
    secondary_pieces,
    piece_target,
    piece_block,
    piece_row,
    piece_column,
    ramp_rate,
    centroid,
    sinc_blocks,
    reference_tile,
    intersection_rows,
):
    tile_count = lax.axis_size("az")
    capacity = max(2, 2 * secondary_pieces.shape[0] // tile_count)
    tables, taps = gather_tables(ramp_rate, centroid, sinc_blocks)
    coregistered, message, lines = resample(
        secondary_pieces,
        piece_target[:, 0],
        piece_block,
        piece_row,
        piece_column,
        tables,
        taps,
        capacity,
    )
    interferogram, diversity = exchange(message, lines, reference_tile, intersection_rows)
    return coregistered, interferogram, diversity


def solution(mesh):
    split = ("dates", "az")
    return jax.shard_map(
        on_device,
        mesh=mesh,
        in_specs=(
            P(split, None, None, None),
            P(split, None),
            P(split),
            P(split),
            P(split),
            P(split, None),
            P(split, None),
            P(),
            P(None, split, None),
            P(split),
        ),
        out_specs=(
            P(split, None, None, None),
            P(None, split, None),
            P(split, None, None),
        ),
        check_vma=False,
    )
```

```python
import functools

import jax
import jax.numpy as jnp
from jax import lax
from jax.experimental import pallas as pl
from jax.experimental.pallas import tpu as pltpu
from jax.sharding import PartitionSpec as P

TILE_ROWS = 256
INTERSECTION = 32
WEIGHT_BLOCKS = 64
GROUP = 16
MATES = 8
VMEM_BYTES = 63 * 1024 * 1024
EXCHANGE_BYTES = 53 * 1024 * 1024
MESH = pl.DeviceIdType.MESH

SIN_FIT = (6.2831807136535645, -41.33925247192383, 81.40833282470703, -71.61119079589844)
COS_FIT = (0.9999932646751404, -19.73573875427246, 64.65997314453125, -78.21002960205078)


def unit_phasor(turns):
    part = turns - jnp.round(turns)
    w = 0.25 - jnp.abs(part)
    w2 = w * w
    even = jnp.full_like(w2, COS_FIT[-1])
    for coeff in COS_FIT[-2::-1]:
        even = even * w2 + coeff
    odd = jnp.full_like(w2, SIN_FIT[-1])
    for coeff in SIN_FIT[-2::-1]:
        odd = odd * w2 + coeff
    return odd * w, jnp.where(part < 0, -even, even)


def resample_kernel(
    target_ref,
    block_ref,
    row_ref,
    col_ref,
    pieces_ref,
    table_ref,
    taps_hbm,
    out_ref,
    message_ref,
    lines_ref,
    deramped_a,
    band_a,
    mixed_a,
    deramped_b,
    band_b,
    mixed_b,
    used,
    target,
    block,
    row,
    col,
    pieces,
    taps_ref,
    fetch_sem,
    pieces_sem,
):
    step = pl.program_id(0)
    width = pieces_ref.shape[3]
    half = width // 2
    fetches = [
        pltpu.make_async_copy(source, scalars, fetch_sem.at[i])
        for i, (source, scalars) in enumerate(
            [
                (target_ref, target),
                (block_ref, block),
                (row_ref, row),
                (col_ref, col),
                (taps_hbm, taps_ref),
            ]
        )
    ]

    def pieces_copy(group):
        part = pl.ds(group * GROUP, GROUP)
        return pltpu.make_async_copy(
            pieces_ref.at[part], pieces.at[part], pieces_sem.at[group]
        )

    @pl.when(step == 0)
    def _():
        for fetch in fetches:
            fetch.start()

        @pl.loop(0, pieces_ref.shape[0] // GROUP)
        def _(group):
            pieces_copy(group).start()

        message_ref[...] = jnp.zeros_like(message_ref)
        band_a[...] = jnp.zeros_like(band_a)
        band_b[...] = jnp.zeros_like(band_b)
        lines_ref[...] = jnp.full_like(lines_ref, -1)

        @pl.loop(0, used.shape[0])
        def _(tile):
            used[tile] = 0

        for fetch in fetches:
            fetch.wait()

    pieces_copy(2 * step).wait()
    pieces_copy(2 * step + 1).wait()

    in_iota = lax.broadcasted_iota(jnp.int32, (16, width), 0).astype(jnp.float32)
    out_iota = lax.broadcasted_iota(jnp.int32, (8, width), 0).astype(jnp.float32)
    band_lane = lax.broadcasted_iota(jnp.int32, (64, 128), 1) // 16
    lane = lax.broadcasted_iota(jnp.int32, (8, half), 1)
    slot_lane = lax.broadcasted_iota(jnp.int32, (1, lines_ref.shape[2]), 1)
    slot_line = slot_lane % 8

    def table_rows(tile):
        return 0.5 * table_ref[tile, 0], table_ref[tile, 1]

    def before(part, i, deramped, band):
        p = (2 * step + part) * GROUP + i
        rate, centre = table_rows(target[p])
        u = (in_iota + (row[p].astype(jnp.float32) - (3.0 + TILE_ROWS / 2))) * (1.0 / TILE_ROWS)
        cosine, sine = unit_phasor((rate * u + centre) * u)
        real = pieces[p, 0].astype(jnp.float32)
        imag = pieces[p, 1].astype(jnp.float32)
        lines = slice(i * 16, i * 16 + 16)
        deramped[lines, 0:width] = (real * cosine + imag * sine).astype(jnp.bfloat16)
        deramped[lines, width : 2 * width] = (imag * cosine - real * sine).astype(jnp.bfloat16)
        taps = taps_ref[block[p]]
        first = i // 8 * 128
        band[i * 64 : i * 64 + 64, first : first + 128] = jnp.where(
            band_lane == i % 8, taps, jnp.zeros_like(taps)
        )


    def after(part, i, mixed):
        p = (2 * step + part) * GROUP + i
        tile = target[p]
        shift0 = col[p] - 3
        sums = [jnp.zeros((8, half), jnp.float32) for _ in range(4)]
        for b in range(8):
            shift = shift0 + b
            turn = lax.rem(half - shift, half)
            place = lane + shift
            inside = (place >= 0) & (place < half)
            above = (shift > 0).astype(jnp.float32)
            below = (shift < 0).astype(jnp.float32)
            lines = slice(i * 64 + b * 8, i * 64 + b * 8 + 8)
            for z in range(2):
                left = pltpu.roll(mixed[lines, z * width : z * width + half], turn, 1)
                right = pltpu.roll(mixed[lines, z * width + half : (z + 1) * width], turn, 1)
                sums[2 * z] = sums[2 * z] + jnp.where(inside, left, right * above)
                sums[2 * z + 1] = sums[2 * z + 1] + jnp.where(inside, right, left * below)
        real = jnp.concatenate(sums[0:2], axis=1)
        imag = jnp.concatenate(sums[2:4], axis=1)
        rate, centre = table_rows(tile)
        start = (
            row[p].astype(jnp.float32)
            + block[p].astype(jnp.float32) * (1.0 / WEIGHT_BLOCKS)
            - TILE_ROWS / 2
        )
        u = (out_iota + start) * (1.0 / TILE_ROWS)
        cosine, sine = unit_phasor((rate * u + centre) * u)
        out_real = real * cosine - imag * sine
        out_imag = imag * cosine + real * sine
        out_ref[part * GROUP + i, 0] = out_real.astype(jnp.bfloat16)
        out_ref[part * GROUP + i, 1] = out_imag.astype(jnp.bfloat16)
        slot = used[tile]
        used[tile] = slot + 1
        message_ref[tile, pl.ds(pl.multiple_of(slot * 16, 16), 16), :] = jnp.concatenate(
            [out_real, out_imag], axis=0
        ).astype(jnp.bfloat16)
        mate, plane = lax.rem(tile, MATES), pl.ds(tile // MATES, 1)
        lines_ref[mate, plane, :] = jnp.where(
            slot_lane // 16 == slot, slot_line + row[p], lines_ref[mate, plane, :]
        )

    def mix(deramped, band, mixed):
        mixed[...] = jnp.dot(band[...], deramped[...], preferred_element_type=jnp.float32)

    for i in range(GROUP):
        before(0, i, deramped_a, band_a)
    mix(deramped_a, band_a, mixed_a)
    for i in range(GROUP):
        before(1, i, deramped_b, band_b)
    mix(deramped_b, band_b, mixed_b)
    for i in range(GROUP):
        after(0, i, mixed_a)
    for i in range(GROUP):
        after(1, i, mixed_b)


def resample(pieces, target, block, row, col, tables, taps, capacity):
    count, _, _, width = pieces.shape
    tiles = tables.shape[0]
    rows = capacity * 16
    line_shape = (MATES, max(8, tiles // MATES), max(128, rows))
    whole = lambda *shape: pl.BlockSpec(shape, lambda g: (0,) * len(shape))
    remote = pl.BlockSpec(memory_space=pltpu.HBM)
    return pl.pallas_call(
        resample_kernel,
        grid_spec=pltpu.PrefetchScalarGridSpec(
            num_scalar_prefetch=0,
            grid=(count // (2 * GROUP),),
            in_specs=[
                *[remote] * 5,
                whole(*tables.shape),
                remote,
            ],
            out_specs=[
                pl.BlockSpec((2 * GROUP, 2, 8, width), lambda g: (g, 0, 0, 0)),
                whole(tiles, rows, width),
                whole(*line_shape),
            ],
            scratch_shapes=[
                *[
                    pltpu.VMEM((GROUP * 16, 2 * width), jnp.bfloat16),
                    pltpu.VMEM((GROUP * 64, GROUP * 16), jnp.bfloat16),
                    pltpu.VMEM((GROUP * 64, 2 * width), jnp.float32),
                ]
                * 2,
                pltpu.SMEM((tiles,), jnp.int32),
                *[pltpu.SMEM((count,), jnp.int32)] * 4,
                pltpu.VMEM(pieces.shape, jnp.bfloat16),
                pltpu.VMEM(taps.shape, jnp.bfloat16),
                pltpu.SemaphoreType.DMA((5,)),
                pltpu.SemaphoreType.DMA((count // GROUP,)),
            ],
        ),
        out_shape=[
            jax.ShapeDtypeStruct((count, 2, 8, width), jnp.bfloat16),
            jax.ShapeDtypeStruct((tiles, rows, width), jnp.bfloat16),
            jax.ShapeDtypeStruct(line_shape, jnp.int32),
        ],
        compiler_params=pltpu.CompilerParams(
            dimension_semantics=("arbitrary",), vmem_limit_bytes=VMEM_BYTES
        ),
        name="resample",
    )(target, block, row, col, pieces, tables, taps)


def gather_kernel(
    n,
    rate_ref,
    centre_ref,
    sinc_ref,
    out_ref,
    taps_ref,
    own,
    got,
    sinc,
    wide,
    fetch_sem,
    send_sem,
    recv_sem,
):
    me = lax.axis_index("az")
    fetches = [
        pltpu.make_async_copy(rate_ref, own.at[0], fetch_sem.at[0]),
        pltpu.make_async_copy(centre_ref, own.at[1], fetch_sem.at[1]),
        pltpu.make_async_copy(sinc_ref, sinc, fetch_sem.at[2]),
    ]
    for fetch in fetches:
        fetch.start()
    barrier = pltpu.get_barrier_semaphore()

    def to_all(k):
        to = lax.rem(me + k, n)
        return pltpu.make_async_remote_copy(
            src_ref=own,
            dst_ref=got.at[me],
            send_sem=send_sem.at[k],
            recv_sem=recv_sem.at[k],
            device_id={"az": to},
            device_id_type=MESH,
        )

    def from_all(k):
        return pltpu.make_async_remote_copy(
            src_ref=own,
            dst_ref=got.at[lax.rem(me - k + n, n)],
            send_sem=send_sem.at[k],
            recv_sem=recv_sem.at[k],
            device_id={"az": lax.rem(me + k, n)},
            device_id_type=MESH,
        )

    @pl.loop(1, n)
    def _(k):
        pl.semaphore_signal(
            barrier, inc=1, device_id={"az": lax.rem(me + k, n)}, device_id_type=MESH
        )

    fetches[0].wait()
    fetches[1].wait()
    got[me] = own[...]
    pl.semaphore_wait(barrier, n - 1)

    @pl.loop(1, n)
    def _(k):
        to_all(k).start()

    fetches[2].wait()
    blocks = sinc_ref.shape[2]
    place = (
        lax.broadcasted_iota(jnp.int32, (8, 128), 1) % 16
        == lax.broadcasted_iota(jnp.int32, (8, 128), 0)
    ).astype(jnp.float32)
    for b in range(8):
        wide[b] = lax.dot_general(
            sinc[:, b, :],
            place,
            (((0,), (0,)), ((), ())),
            preferred_element_type=jnp.float32,
        )

    @pl.loop(0, blocks)
    def _(block):
        for b in range(0, 8, 2):
            pair = jnp.concatenate(
                [
                    pltpu.roll(
                        jnp.broadcast_to(wide[b + e, pl.ds(block, 1), :], (8, 128)),
                        0,
                        1,
                        stride=1,
                        stride_axis=0,
                    )
                    for e in range(2)
                ],
                axis=0,
            ).astype(jnp.bfloat16)
            taps_ref[block, b * 8 : b * 8 + 16, :] = pair

    @pl.loop(1, n)
    def _(k):
        from_all(k).wait_recv()

    out_ref[...] = got[...]

    @pl.loop(1, n)
    def _(k):
        to_all(k).wait_send()


def gather_tables(rate, centre, sinc_blocks):
    n = lax.axis_size("az")
    width = rate.shape[1]
    blocks = sinc_blocks.shape[0]
    return pl.pallas_call(
        functools.partial(gather_kernel, n),
        in_specs=[pl.BlockSpec(memory_space=pltpu.HBM)] * 3,
        out_specs=[pl.BlockSpec(memory_space=pltpu.VMEM)] * 2,
        out_shape=[
            jax.ShapeDtypeStruct((n, 2, 1, width), jnp.float32),
            jax.ShapeDtypeStruct((blocks, 64, 128), jnp.bfloat16),
        ],
        scratch_shapes=[
            pltpu.VMEM((2, 1, width), jnp.float32),
            pltpu.VMEM((n, 2, 1, width), jnp.float32),
            pltpu.VMEM((8, 8, blocks), jnp.float32),
            pltpu.VMEM((8, blocks, 128), jnp.float32),
            pltpu.SemaphoreType.DMA((3,)),
            pltpu.SemaphoreType.DMA((n,)),
            pltpu.SemaphoreType.DMA((n,)),
        ],
        compiler_params=pltpu.CompilerParams(
            collective_id=1, has_side_effects=True, vmem_limit_bytes=VMEM_BYTES
        ),
        name="gather_tables",
    )(rate, centre, jnp.transpose(sinc_blocks, (1, 2, 0)))


def exchange_kernel(
    n,
    length_ref,
    message_ref,
    lines_hbm,
    tile_hbm,
    out_ref,
    sum_ref,
    lines_ref,
    tile_ref,
    own_sem,
    got,
    got_lines,
    part,
    got_part,
    total,
    tail,
    previous,
    send_sem,
    recv_sem,
    lines_send_sem,
    lines_recv_sem,
    part_send_sem,
    part_recv_sem,
    tail_sem,
):
    me = lax.axis_index("az")
    height = tile_hbm.shape[1]
    rows, width = message_ref.shape[1:]
    m = n // MATES
    lines_fetch = pltpu.make_async_copy(lines_hbm, lines_ref, own_sem.at[0])
    tile_fetch = pltpu.make_async_copy(tile_hbm, tile_ref, own_sem.at[1])
    lines_fetch.start()
    tile_fetch.start()
    high, low = me // MATES, lax.rem(me, MATES)

    def mate(e):
        return high * MATES + lax.rem(low + e, MATES)

    def peer(k):
        return lax.rem(high + k, m) * MATES + low

    def lines_copy(e):
        return pltpu.make_async_remote_copy(
            src_ref=lines_ref.at[lax.rem(low + e, MATES)],
            dst_ref=got_lines.at[e],
            send_sem=lines_send_sem.at[e],
            recv_sem=lines_recv_sem.at[e],
            device_id={"az": mate(e)},
            device_id_type=MESH,
        )

    def data_copy(k, e):
        tile = lax.rem(high + k, m) * MATES + lax.rem(low + e, MATES)
        return pltpu.make_async_remote_copy(
            src_ref=message_ref.at[tile],
            dst_ref=got.at[k, e],
            send_sem=send_sem.at[k, e],
            recv_sem=recv_sem.at[k, e],
            device_id={"az": mate(e)},
            device_id_type=MESH,
        )

    def own_copy(k):
        return pltpu.make_async_copy(message_ref.at[peer(k)], got.at[k, 0], own_sem.at[2 + k])

    def part_copy(k):
        return pltpu.make_async_remote_copy(
            src_ref=part.at[k],
            dst_ref=got_part.at[k],
            send_sem=part_send_sem.at[k],
            recv_sem=part_recv_sem.at[k],
            device_id={"az": peer(k)},
            device_id_type=MESH,
        )

    tail_copy = pltpu.make_async_remote_copy(
        src_ref=tail,
        dst_ref=previous,
        send_sem=tail_sem.at[0],
        recv_sem=tail_sem.at[1],
        device_id={"az": lax.rem(me + 1, n)},
        device_id_type=MESH,
    )

    @pl.loop(0, m)
    def _(k):
        own_copy(k).start()

    barrier = pltpu.get_barrier_semaphore()
    for e in range(1, MATES):
        pl.semaphore_signal(barrier, inc=1, device_id={"az": mate(e)}, device_id_type=MESH)

    @pl.loop(1, m)
    def _(k):
        pl.semaphore_signal(barrier, inc=1, device_id={"az": peer(k)}, device_id_type=MESH)

    @pl.when(low == 0)
    def _():
        pl.semaphore_signal(
            barrier, inc=1, device_id={"az": lax.rem(me + n - 1, n)}, device_id_type=MESH
        )

    @pl.when(me == 0)
    def _():
        previous[...] = jnp.zeros_like(previous)

    pl.semaphore_wait(barrier, MATES - 1 + m - 1 + low // (MATES - 1))

    lines_fetch.wait()
    for e in range(1, MATES):
        lines_copy(e).start()

    def order(j):
        return 1 + lax.rem(j + m // 2 - 1, m - 1) if m > 1 else 0

    for e in range(1, MATES):
        data_copy(order(0), e).start()

    def as_bf16(value):
        return value.astype(jnp.float32).astype(jnp.bfloat16)

    wanted = as_bf16(lax.broadcasted_iota(jnp.int32, (height, rows), 0))
    channel = lax.broadcasted_iota(jnp.int32, (rows, width), 0) // 8 % 2
    is_imag = as_bf16(channel)
    is_real = as_bf16(1 - channel)

    def placed(lines, data):
        one = jnp.ones((), jnp.bfloat16)
        pick = jnp.where(wanted == as_bf16(lines), one, jnp.zeros_like(one))
        both = jnp.concatenate([data * is_real, data * is_imag], axis=1)
        return jnp.dot(pick, both, preferred_element_type=jnp.float32)

    def summed(k):
        plane = lax.rem(high + k, m)
        own_copy(k).wait()
        result = placed(lines_ref[low, pl.ds(plane, 1), 0:rows], got[k, 0])
        for e in range(1, MATES):
            data_copy(k, e).wait_recv()
            result = result + placed(got_lines[e, pl.ds(plane, 1), 0:rows], got[k, e])
        return result

    for e in range(1, MATES):
        lines_copy(e).wait_recv()

    @pl.loop(0, m - 1)
    def _(j):
        k = order(j)
        following = jnp.where(j + 1 == m - 1, 0, order(j + 1))
        for e in range(1, MATES):
            data_copy(k, e).wait_send()
            data_copy(following, e).start()
        part[k] = summed(k).astype(jnp.bfloat16)
        part_copy(k).start()

    total[...] = summed(0)

    @pl.loop(0, m - 1)
    def _(j):
        k = order(j)
        part_copy(k).wait_recv()
        total[...] += got_part[k].astype(jnp.float32)

    tile_fetch.wait()
    ref_real, ref_imag = tile_ref[0], tile_ref[1]
    got_real, got_imag = total[:, 0:width], total[:, width : 2 * width]
    last = slice(height - INTERSECTION, height)
    tail[0] = ref_real[last] * got_real[last] + ref_imag[last] * got_imag[last]
    tail[1] = ref_imag[last] * got_real[last] - ref_real[last] * got_imag[last]

    @pl.when(me < n - 1)
    def _():
        tail_copy.start()

    out_ref[0] = ref_real * got_real + ref_imag * got_imag
    out_ref[1] = ref_imag * got_real - ref_real * got_imag

    length = length_ref[0]
    apart = lax.broadcasted_iota(
        jnp.int32, (INTERSECTION, INTERSECTION), 0
    ) - lax.broadcasted_iota(jnp.int32, (INTERSECTION, INTERSECTION), 1)
    shifter = (apart == INTERSECTION - length).astype(jnp.float32)
    head = [
        jnp.dot(
            shifter,
            out_ref[z, 0:INTERSECTION, :],
            precision=lax.Precision.HIGHEST,
            preferred_element_type=jnp.float32,
        )
        for z in range(2)
    ]

    @pl.when(me > 0)
    def _():
        tail_copy.wait_recv()

    before = [previous[z] for z in range(2)]
    scale = 1.0 / length.astype(jnp.float32)
    sum_ref[0, 0:1, :] = scale * jnp.sum(
        head[0] * before[0] + head[1] * before[1], axis=0, keepdims=True
    )
    sum_ref[0, 1:2, :] = scale * jnp.sum(
        head[1] * before[0] - head[0] * before[1], axis=0, keepdims=True
    )

    for e in range(1, MATES):
        lines_copy(e).wait_send()

    for e in range(1, MATES):
        data_copy(0, e).wait_send()

    @pl.loop(1, m)
    def _(k):
        part_copy(k).wait_send()

    @pl.when(me < n - 1)
    def _():
        tail_copy.wait_send()


def exchange(message, lines, tile, length):
    n, rows, width = message.shape
    height = tile.shape[1]
    m = n // MATES
    dma = pltpu.SemaphoreType.DMA
    return pl.pallas_call(
        functools.partial(exchange_kernel, n),
        in_specs=[pl.BlockSpec(memory_space=pltpu.SMEM)]
        + [pl.BlockSpec(memory_space=pltpu.HBM)] * 3,
        out_specs=[pl.BlockSpec(memory_space=pltpu.VMEM)] * 2,
        out_shape=[
            jax.ShapeDtypeStruct(tile.shape, jnp.float32),
            jax.ShapeDtypeStruct((1, 2, width), jnp.float32),
        ],
        scratch_shapes=[
            pltpu.VMEM(lines.shape, jnp.int32),
            pltpu.VMEM(tile.shape, jnp.float32),
            dma((2 + m,)),
            pltpu.VMEM((m, MATES, rows, width), jnp.bfloat16),
            pltpu.VMEM(lines.shape, jnp.int32),
            pltpu.VMEM((m, height, 2 * width), jnp.bfloat16),
            pltpu.VMEM((m, height, 2 * width), jnp.bfloat16),
            pltpu.VMEM((height, 2 * width), jnp.float32),
            pltpu.VMEM((2, INTERSECTION, width), jnp.float32),
            pltpu.VMEM((2, INTERSECTION, width), jnp.float32),
            dma((m, MATES)),
            dma((m, MATES)),
            dma((MATES,)),
            dma((MATES,)),
            dma((m,)),
            dma((m,)),
            dma((2,)),
        ],
        compiler_params=pltpu.CompilerParams(
            collective_id=0, has_side_effects=True, vmem_limit_bytes=EXCHANGE_BYTES
        ),
        name="exchange",
    )(length, message, lines, tile)


def on_device(
    secondary_pieces,
    piece_target,
    piece_block,
    piece_row,
    piece_column,
    ramp_rate,
    centroid,
    sinc_blocks,
    reference_tile,
    intersection_rows,
):
    tile_count = lax.axis_size("az")
    capacity = max(2, 2 * secondary_pieces.shape[0] // tile_count)
    tables, taps = gather_tables(ramp_rate, centroid, sinc_blocks)
    coregistered, message, lines = resample(
        secondary_pieces,
        piece_target[:, 0],
        piece_block,
        piece_row,
        piece_column,
        tables,
        taps,
        capacity,
    )
    interferogram, diversity = exchange(message, lines, reference_tile, intersection_rows)
    return coregistered, interferogram, diversity


def solution(mesh):
    split = ("dates", "az")
    return jax.shard_map(
        on_device,
        mesh=mesh,
        in_specs=(
            P(split, None, None, None),
            P(split, None),
            P(split),
            P(split),
            P(split),
            P(split, None),
            P(split, None),
            P(),
            P(None, split, None),
            P(split),
        ),
        out_specs=(
            P(split, None, None, None),
            P(None, split, None),
            P(split, None, None),
        ),
        check_vma=False,
    )
```
